32 devices in a mesh: grp: 4 (over y, core), dev: 8 (over z, x).
Axes of the slice: x: 2, y: 2, z: 4, core: 2. Of those that a mesh axis runs over, the one named last changes fastest.
Arguments:
- basis_old: float32 [128, 524288], P(None, ('grp', 'dev')), as said below
- values_old: float32 [128], replicated, may hold values from 1 to 4
- snapshots: float32 [2, 64, 524288], P(None, None, ('grp', 'dev'))
- wet_counts: int32 [32], P(('grp', 'dev')), may hold values from 1 to 128, as said below
Outputs:
- basis_new: float32 [128, 524288], P(None, ('grp', 'dev'))
- values_new: float32 [128], replicated
The draws below stay inside these ranges and needn't reach their ends.
Inputs may be any that keep to these rules, and one draw needn't show every extreme that they name: `wet_counts`: every device has at least one wet block, and some device has all 128 blocks wet. basis_old is zero on every cell that wet_mask marks dry.
All inputs are finite; a program needn't handle non-finite values.
Results may differ from the reference program's by a relative error of at most 0.0003.
Values sent between devices are 32-bit elements; how exact they have to be, the bound alone decides.
A program may use at most 128 MiB of HBM per device.

```python
import math
import jax
import jax.numpy as jnp
from jax import lax

K = 128
B = 64
BLOCK = 128
BLK_DEV = 128
ROWS_DEV = 16384
SHARDS = 32
ROWS = 524288
UPDATES = 2
SWEEPS = 3


def shared_modes(key):
    return jax.random.normal(jax.random.fold_in(key, 11), (K, ROWS), jnp.float32)


def shared_counts(key):
    counts = jax.random.randint(jax.random.fold_in(key, 31), (SHARDS,), 1, BLK_DEV + 1, jnp.int32)
    chosen = jax.random.randint(jax.random.fold_in(key, 32), (), 0, SHARDS, jnp.int32)
    return counts.at[chosen].set(BLK_DEV)


def shared_mask(key):
    counts = shared_counts(key)
    cells = jnp.arange(ROWS, dtype=jnp.int32)
    owners = (cells // ROWS_DEV).astype(jnp.int32)
    blocks = (cells % ROWS_DEV // BLOCK).astype(jnp.int32)
    return (blocks < jnp.take(counts, owners)).astype(jnp.float32)


def draw_basis_old(key, part):
    return shared_modes(key) * shared_mask(key)[None, :]


def draw_snapshots(key, part):
    modes = shared_modes(key)
    coeff = jax.random.normal(jax.random.fold_in(key, 21), (UPDATES, K, B), jnp.float32)
    mode_scale = jnp.exp(jax.random.uniform(jax.random.fold_in(key, 22), (1, K, 1), jnp.float32, math.log(0.3), math.log(3.0)))
    coeff = coeff * mode_scale
    signal = jnp.einsum('ukb,km->ubm', coeff, modes)
    col_scale = jnp.exp(jax.random.uniform(jax.random.fold_in(key, 25), (UPDATES, B, 1), jnp.float32, 0.0, math.log(3.0)))
    noise = jax.random.normal(jax.random.fold_in(key, 24), (UPDATES, B, ROWS), jnp.float32)
    row_scale = jnp.exp(jax.random.uniform(jax.random.fold_in(key, 23), (ROWS,), jnp.float32, 0.0, math.log(10.0)))
    return (signal + 0.5 * noise * row_scale[None, None, :]) * col_scale


def draw_wet_counts(key, part):
    return shared_counts(key)


def setup_inputs(seed: int = 0) -> dict:
    key_of = jax.random.split(jax.random.key(seed), 5)
    return {
        "basis_old": draw_basis_old(jax.random.fold_in(key_of[4], 71), 0),
        "values_old": jnp.clip(jnp.exp(jax.random.uniform(key_of[1], (K,), jnp.float32, math.log(1.0), math.log(4.0))), 1.0, 4.0),
        "snapshots": draw_snapshots(jax.random.fold_in(key_of[4], 71), 0),
        "wet_counts": draw_wet_counts(jax.random.fold_in(key_of[4], 71), 0),
    }


def matmul_nn(left_op, right_op):
    return jnp.dot(left_op.astype(jnp.float32), right_op.astype(jnp.float32), precision=lax.Precision.HIGHEST, preferred_element_type=jnp.float32)

def matmul_nt(left_op, right_op):
    return lax.dot_general(left_op.astype(jnp.float32), right_op.astype(jnp.float32), (((1,), (1,)), ((), ())), precision=lax.Precision.HIGHEST, preferred_element_type=jnp.float32)

def matmul_tn(left_op, right_op):
    return lax.dot_general(left_op.astype(jnp.float32), right_op.astype(jnp.float32), (((0,), (0,)), ((), ())), precision=lax.Precision.HIGHEST, preferred_element_type=jnp.float32)

def assemble(values, project, factor):
    upper_block = jnp.concatenate([jnp.diag(values), project], 1)
    bottom = jnp.concatenate([jnp.zeros((factor.shape[0], values.shape[0]), jnp.float32), factor.T], 1)
    return jnp.concatenate([upper_block, bottom], 0)

def refine(core_matrix, rank_width):
    frame_now = jnp.eye(core_matrix.shape[0], rank_width, dtype=jnp.float32)
    for repeat in range(SWEEPS):
        grown_cols = matmul_nn(core_matrix, matmul_tn(core_matrix, frame_now))
        lower_part = jnp.linalg.cholesky(matmul_tn(grown_cols, grown_cols))
        frame_now = jax.scipy.linalg.solve_triangular(lower_part, grown_cols.T, lower=True).T
    return frame_now

def reference(basis_old, values_old, snapshots, wet_counts):
    cells = jnp.arange(ROWS, dtype=jnp.int32)
    owners = (cells // ROWS_DEV).astype(jnp.int32)
    blocks = (cells % ROWS_DEV // BLOCK).astype(jnp.int32)
    wet_mask = (blocks < jnp.take(wet_counts, owners)).astype(jnp.float32)
    wet_total = jnp.sum(wet_counts).astype(jnp.float32) * BLOCK
    rank_width = basis_old.shape[0]

    def update_one(state_pair, snapshot):
        current, values = state_pair
        columns = snapshot * wet_mask[None, :]
        project = matmul_nt(current, columns) / wet_total
        remainder = columns - matmul_tn(project, current)
        gram = matmul_nt(remainder, remainder) / wet_total
        factor = jnp.linalg.cholesky(gram)
        fresh_rows = jax.scipy.linalg.solve_triangular(factor, remainder, lower=True)
        core_matrix = assemble(values, project, factor)
        frame_now = refine(core_matrix, rank_width)
        stacked = jnp.concatenate([current, fresh_rows], 0)
        new_basis = matmul_tn(frame_now, stacked)
        rotated = matmul_tn(frame_now, core_matrix)
        new_values = jnp.sqrt(lax.optimization_barrier(jnp.sum(rotated * rotated, axis=1)))
        return ((new_basis, new_values), None)
    (current, values), _ = lax.scan(update_one, (basis_old, values_old), snapshots)
    return (current, values)
```

```python
import functools

import jax
import jax.numpy as jnp
from jax import lax
from jax.experimental import pallas as pl
from jax.experimental.pallas import tpu as pltpu
from jax.sharding import PartitionSpec as P

BLOCK = 128
SWEEPS = 3
PANEL = 16
SUB = 8
TILE = 2048
MESH = pl.DeviceIdType.MESH
F32 = jnp.float32
BF16 = jnp.bfloat16


def dot_full(left_op, right_op, dims):
    return lax.dot_general(
        left_op, right_op, (dims, ((), ())), precision=lax.Precision.HIGHEST, preferred_element_type=F32
    )


def nn(left_op, right_op):
    return dot_full(left_op, right_op, ((1,), (0,)))


def nt(left_op, right_op):
    return dot_full(left_op, right_op, ((1,), (1,)))


def tn(left_op, right_op):
    return dot_full(left_op, right_op, ((0,), (0,)))


def dot_half(left_op, right_op, dims):
    return lax.dot_general(left_op, right_op, (dims, ((), ())), preferred_element_type=F32)


def split_two(x):
    high = x.astype(BF16)
    return high, (x - high.astype(F32)).astype(BF16)


def split_three(x):
    high = x.astype(BF16)
    rest = x - high.astype(F32)
    mid = rest.astype(BF16)
    return high, mid, (rest - mid.astype(F32)).astype(BF16)


def masked_stack(counts_ref, basis_ref, snaps_ref, step):
    rank_width, tile = basis_ref.shape
    snaps = jnp.concatenate([snaps_ref[t] for t in range(snaps_ref.shape[0])], 0)
    cell = step * tile + lax.broadcasted_iota(jnp.int32, snaps.shape, 1)
    snaps = jnp.where(cell < counts_ref[0] * BLOCK, snaps, 0.0)
    return jnp.concatenate([basis_ref[...], snaps], 0)


def gram_kernel(counts_ref, basis_ref, snaps_ref, out_ref, main, cross):
    step = pl.program_id(0)
    rank_width = basis_ref.shape[0]

    @pl.when(step == 0)
    def _():
        main[...] = jnp.zeros_like(main)
        cross[...] = jnp.zeros_like(cross)

    high, low = split_two(masked_stack(counts_ref, basis_ref, snaps_ref, step))
    dims = ((1,), (1,))
    main[...] += dot_half(high, high, dims) + dot_half(low, low, dims)
    cross[...] += dot_half(high, low, dims)

    @pl.when(step == pl.num_programs(0) - 1)
    def _():
        total = main[...] + cross[...] + cross[...].T
        parts = total.shape[0] // rank_width
        row = 0
        for i in range(parts):
            for j in range(i + 1):
                block = total[
                    i * rank_width : (i + 1) * rank_width, j * rank_width : (j + 1) * rank_width
                ]
                if i == 0:
                    spot = (lax.broadcasted_iota(jnp.int32, block.shape, 0) == 0) & (
                        lax.broadcasted_iota(jnp.int32, block.shape, 1) == rank_width - 1
                    )
                    block = jnp.where(spot, counts_ref[0].astype(F32), block)
                out_ref[row : row + rank_width, :] = block
                row += rank_width
        if row < out_ref.shape[0]:
            out_ref[row:, :] = jnp.zeros((out_ref.shape[0] - row, out_ref.shape[1]), F32)


def sum_kernel(
    groups, near, far, in_ref, out_ref, near_buf, far_buf, all_buf,
    near_send, near_recv, far_send, far_recv, back_send, back_recv,
):
    grp, dev = lax.axis_index("grp"), lax.axis_index("dev")
    level, across = dev // near, lax.rem(dev, near)
    members = groups * near
    me = grp * near + across
    chunk = in_ref.shape[0] // members

    def member(offset):
        rank = lax.rem(me + offset, members)
        return rank, (rank // near, level * near + lax.rem(rank, near))

    def along(offset):
        return (grp, lax.rem(level + offset, far) * near + across)

    barrier = pltpu.get_barrier_semaphore()
    for offset in range(1, members):
        pl.semaphore_signal(barrier, inc=1, device_id=member(offset)[1], device_id_type=MESH)
    for offset in range(1, far):
        pl.semaphore_signal(barrier, inc=1, device_id=along(offset), device_id_type=MESH)
    pl.semaphore_wait(barrier, members - 1 + far - 1)

    copies = []
    for offset in range(1, members):
        rank, where = member(offset)
        copies.append(
            pltpu.make_async_remote_copy(
                src_ref=in_ref.at[pl.ds(pl.multiple_of(rank * chunk, SUB), chunk)],
                dst_ref=near_buf.at[offset],
                send_sem=near_send.at[offset],
                recv_sem=near_recv.at[offset],
                device_id=where,
                device_id_type=MESH,
            )
        )
        copies[-1].start()
    mine = pl.ds(pl.multiple_of(me * chunk, SUB), chunk)
    total = in_ref[mine, :]
    for offset, copy in enumerate(copies, 1):
        copy.wait_recv()
        total = total + near_buf[offset]
    far_buf[level] = total
    sends = copies

    copies = []
    for offset in range(1, far):
        copies.append(
            pltpu.make_async_remote_copy(
                src_ref=far_buf.at[level],
                dst_ref=far_buf.at[level],
                send_sem=far_send.at[offset],
                recv_sem=far_recv.at[offset],
                device_id=along(offset),
                device_id_type=MESH,
            )
        )
        copies[-1].start()
    for copy in copies:
        copy.wait_recv()
    sends = sends + copies
    total = far_buf[0]
    for other in range(1, far):
        total = total + far_buf[other]
    all_buf[mine, :] = total

    copies = []
    for offset in range(1, members):
        copies.append(
            pltpu.make_async_remote_copy(
                src_ref=all_buf.at[mine],
                dst_ref=all_buf.at[mine],
                send_sem=back_send.at[offset],
                recv_sem=back_recv.at[offset],
                device_id=member(offset)[1],
                device_id_type=MESH,
            )
        )
        copies[-1].start()
    for copy in copies:
        copy.wait_recv()
    for copy in sends + copies:
        copy.wait_send()
    out_ref[...] = all_buf[...]


def eliminate(panel, start):
    diagonal, arrays = panel
    halves = PANEL // SUB
    lanes = diagonal.shape[1]
    cols = [
        [
            jnp.broadcast_to(diagonal[h * SUB : (h + 1) * SUB, start + j : start + j + 1], (SUB, lanes))
            for h in range(halves)
        ]
        for j in range(PANEL)
    ]
    work = [[a[h * SUB : (h + 1) * SUB, :] for h in range(halves)] for a in arrays]
    row = lax.broadcasted_iota(jnp.int32, (SUB, lanes), 0)
    pivots = [jnp.ones((SUB, lanes), F32) for _ in range(halves)]
    for j in range(PANEL):
        half, sub = j // SUB, j % SUB
        pivot = jnp.broadcast_to(cols[j][half][sub : sub + 1, :], (SUB, lanes))
        pivots[half] = jnp.where(row == sub, pivot, pivots[half])
        inverse = 1.0 / pivot
        scaled = {
            h: (cols[j][h] * inverse if h > half else jnp.where(row > sub, cols[j][h] * inverse, 0.0))
            for h in range(half, halves)
        }
        for target in cols[j + 1 :] + work:
            lead = jnp.broadcast_to(target[half][sub : sub + 1, :], (SUB, lanes))
            for h in range(half, halves):
                target[h] = target[h] - scaled[h] * lead
    out = []
    scales = []
    for h in range(halves):
        guess = lax.rsqrt(pivots[h])
        scales.append(guess * (1.5 - 0.5 * pivots[h] * guess * guess))
    for target in work:
        out.append(jnp.concatenate([target[h] * scales[h] for h in range(halves)], 0))
    return out


def outer_rows(rows, first):
    high, mid, low = split_three(rows)
    left = jnp.concatenate([high, high, mid, high, mid, low], 0)
    right = jnp.concatenate([high, mid, high, low, mid, high], 0)
    return dot_half(left, right, ((0,), (0,)))[first:, :]


def lower_inverse(ref, size):
    for start in range(0, size, PANEL):
        stop = start + PANEL
        rows = ref[start:stop, :]
        lane = lax.broadcasted_iota(jnp.int32, rows.shape, 1)
        sub = lax.broadcasted_iota(jnp.int32, rows.shape, 0)
        inside = (lane >= start) & (lane < stop)
        eye = (lane == sub + start).astype(F32)
        (rows,) = eliminate((rows, [jnp.where(inside, eye, rows)]), start)
        ref[start:stop, :] = rows
        if stop < size:
            rest = ref[stop:, :]
            lane = lax.broadcasted_iota(jnp.int32, rest.shape, 1)
            rest = jnp.where((lane >= start) & (lane < stop), 0.0, rest)
            masked = rows
            ref[stop:, :] = rest - outer_rows(masked, stop)[: size - stop, :]


def factor_and_inverse(ref, size):
    for start in range(0, size, PANEL):
        stop = start + PANEL
        rows = ref[start:stop, :]
        (rows,) = eliminate((rows, [rows]), start)
        ref[start:stop, :] = rows
        if stop < size:
            ref[stop:, :] = ref[stop:, :] - outer_rows(rows, stop)[: size - stop, :]


def core_kernel(batch, updates, sum_ref, values_ref, coeff_ref, new_values_ref, gram, core, square, frame, big, small):
    rank = values_ref.shape[1]
    width = gram.shape[0]
    rows = lax.broadcasted_iota(jnp.int32, (rank, rank), 0)
    lanes = lax.broadcasted_iota(jnp.int32, (rank, rank), 1)
    eye = rows == lanes
    count = sum_ref[0:1, rank - 1 : rank]
    wet_total = count * BLOCK
    parts = width // rank
    row = 0
    for i in range(parts):
        for j in range(i + 1):
            block = sum_ref[row : row + rank, :]
            row += rank
            if i == 0:
                block = jnp.where((rows == 0) & (lanes == rank - 1), block.T, block)
            gram[i * rank : (i + 1) * rank, j * rank : (j + 1) * rank] = block
            if i != j:
                gram[j * rank : (j + 1) * rank, i * rank : (i + 1) * rank] = block.T

    wide_rows = lax.broadcasted_iota(jnp.int32, (rank, width), 0)
    wide_lanes = lax.broadcasted_iota(jnp.int32, (rank, width), 1)
    start_frame = (wide_rows == wide_lanes).astype(F32)
    coeff_ref[...] = start_frame
    core[...] = jnp.zeros_like(core)
    diag = jnp.where(eye, values_ref[...], 0.0)

    batch_rows = lax.broadcasted_iota(jnp.int32, (batch, width), 0)
    batch_lanes = lax.broadcasted_iota(jnp.int32, (batch, width), 1)
    small_rows = lax.broadcasted_iota(jnp.int32, (batch, batch), 0)
    small_lanes = lax.broadcasted_iota(jnp.int32, (batch, batch), 1)

    for index in range(updates):
        coeff = coeff_ref[...]
        first = rank + index * batch
        projected = gram[:rank, :] if index == 0 else nn(coeff, gram[...])
        project = projected[:, first : first + batch] / wet_total
        picker = (batch_lanes == first + batch_rows).astype(F32)
        remain = picker - tn(project, coeff)
        small[:, :batch] = nt(nn(remain, gram[...]), remain) / wet_total
        small[:, batch:] = (small_rows == small_lanes).astype(F32)
        factor_and_inverse(small, batch)
        factor_t = jnp.where(small_lanes >= small_rows, small[:, :batch], 0.0)
        fresh = nn(small[:, batch:], remain)
        core[:rank, :rank] = diag
        core[:rank, rank : rank + batch] = project
        core[rank : rank + batch, rank : rank + batch] = factor_t
        square[...] = nt(core[...], core[...])
        frame[...] = start_frame

        def sweep(step, carry):
            grown = nn(frame[...], square[...])
            big[...] = nt(grown, grown)
            lower_inverse(big, rank)
            inverse = jnp.where(lanes <= rows, big[...], 0.0)
            frame[...] = nn(inverse, grown)
            return carry

        lax.fori_loop(0, SWEEPS, sweep, 0)
        frame_now = frame[...]
        rotated = nn(frame_now, core[...])
        lengths = jnp.sqrt(jnp.sum(rotated * rotated, axis=1, keepdims=True))
        diag = jnp.where(eye, lengths, 0.0)
        coeff_ref[...] = nn(frame_now[:, :rank], coeff) + nn(frame_now[:, rank : rank + batch], fresh)
    new_values_ref[...] = jnp.sum(diag, axis=0, keepdims=True)


def apply_kernel(counts_ref, coeff_ref, basis_ref, snaps_ref, out_ref):
    rank = basis_ref.shape[0]
    high, low = split_two(masked_stack(counts_ref, basis_ref, snaps_ref, pl.program_id(0)))
    coeff_high, coeff_low = split_two(coeff_ref[...])
    dims = ((1,), (0,))
    both = dot_half(jnp.concatenate([coeff_high, coeff_low], 0), high, dims)
    out_ref[...] = both[:rank, :] + (both[rank:, :] + dot_half(coeff_high, low, dims))


def per_device(groups, devs, basis_old, values_old, snapshots, wet_counts):
    rank, cells = basis_old.shape
    updates, batch = snapshots.shape[0], snapshots.shape[1]
    width = rank + updates * batch
    near = 1
    while (2 * near) * (2 * near) <= devs and devs % (2 * near) == 0:
        near *= 2
    far = devs // near
    members = groups * near
    parts = width // rank
    rows = rank * parts * (parts + 1) // 2
    chunk = -(-rows // (members * SUB)) * SUB
    padded = chunk * members
    tile = min(TILE, cells)

    in_specs = [
        pl.BlockSpec(memory_space=pltpu.SMEM),
        pl.BlockSpec((rank, tile), lambda i: (0, i)),
        pl.BlockSpec((updates, batch, tile), lambda i: (0, 0, i)),
    ]
    vmem = pl.BlockSpec(memory_space=pltpu.VMEM)
    local = pl.pallas_call(
        gram_kernel,
        grid=(cells // tile,),
        out_shape=jax.ShapeDtypeStruct((padded, rank), F32),
        in_specs=in_specs,
        out_specs=pl.BlockSpec((padded, rank), lambda i: (0, 0)),
        scratch_shapes=[pltpu.VMEM((width, width), F32)] * 2,
        compiler_params=pltpu.CompilerParams(vmem_limit_bytes=48 << 20),
    )(wet_counts, basis_old, snapshots)

    summed = pl.pallas_call(
        functools.partial(sum_kernel, groups, near, far),
        out_shape=jax.ShapeDtypeStruct((padded, rank), F32),
        in_specs=[vmem],
        out_specs=vmem,
        scratch_shapes=[
            pltpu.VMEM((members, chunk, rank), F32),
            pltpu.VMEM((far, chunk, rank), F32),
            pltpu.VMEM((padded, rank), F32),
            pltpu.SemaphoreType.DMA((members,)),
            pltpu.SemaphoreType.DMA((members,)),
            pltpu.SemaphoreType.DMA((far,)),
            pltpu.SemaphoreType.DMA((far,)),
            pltpu.SemaphoreType.DMA((members,)),
            pltpu.SemaphoreType.DMA((members,)),
        ],
        compiler_params=pltpu.CompilerParams(collective_id=0, has_side_effects=True),
    )(local)

    coeff, values = pl.pallas_call(
        functools.partial(core_kernel, batch, updates),
        out_shape=(
            jax.ShapeDtypeStruct((rank, width), F32),
            jax.ShapeDtypeStruct((1, rank), F32),
        ),
        in_specs=[vmem, vmem],
        out_specs=(vmem, vmem),
        scratch_shapes=[
            pltpu.VMEM((width, width), F32),
            pltpu.VMEM((width, width), F32),
            pltpu.VMEM((width, width), F32),
            pltpu.VMEM((rank, width), F32),
            pltpu.VMEM((rank, rank), F32),
            pltpu.VMEM((batch, 2 * batch), F32),
        ],
        compiler_params=pltpu.CompilerParams(vmem_limit_bytes=48 << 20),
    )(summed, values_old.reshape(1, rank))

    basis_new = pl.pallas_call(
        apply_kernel,
        grid=(cells // tile,),
        out_shape=jax.ShapeDtypeStruct((rank, cells), F32),
        in_specs=[
            in_specs[0],
            pl.BlockSpec((rank, width), lambda i: (0, 0)),
            in_specs[1],
            in_specs[2],
        ],
        out_specs=pl.BlockSpec((rank, tile), lambda i: (0, i)),
        compiler_params=pltpu.CompilerParams(vmem_limit_bytes=48 << 20),
    )(wet_counts, coeff, basis_old, snapshots)
    return basis_new, values.reshape(rank)


def solution(mesh):
    return jax.shard_map(
        functools.partial(per_device, mesh.shape["grp"], mesh.shape["dev"]),
        mesh=mesh,
        in_specs=(P(None, ("grp", "dev")), P(), P(None, None, ("grp", "dev")), P(("grp", "dev"))),
        out_specs=(P(None, ("grp", "dev")), P()),
        check_vma=False,
    )
```

```python
import functools

import jax
import jax.numpy as jnp
from jax import lax
from jax.experimental import pallas as pl
from jax.experimental.pallas import tpu as pltpu
from jax.sharding import PartitionSpec as P

BLOCK = 128
SWEEPS = 3
PANEL = 32
SUB = 8
TILE = 2048
MESH = pl.DeviceIdType.MESH
F32 = jnp.float32
BF16 = jnp.bfloat16


def dot_full(left_op, right_op, dims):
    return lax.dot_general(
        left_op, right_op, (dims, ((), ())), precision=lax.Precision.HIGHEST, preferred_element_type=F32
    )


def nn(left_op, right_op):
    return dot_full(left_op, right_op, ((1,), (0,)))


def nt(left_op, right_op):
    return dot_full(left_op, right_op, ((1,), (1,)))


def tn(left_op, right_op):
    return dot_full(left_op, right_op, ((0,), (0,)))


def dot_half(left_op, right_op, dims):
    return lax.dot_general(left_op, right_op, (dims, ((), ())), preferred_element_type=F32)


def split_two(x):
    high = x.astype(BF16)
    return high, (x - high.astype(F32)).astype(BF16)


def split_three(x):
    high = x.astype(BF16)
    rest = x - high.astype(F32)
    mid = rest.astype(BF16)
    return high, mid, (rest - mid.astype(F32)).astype(BF16)


def masked_stack(counts_ref, basis_ref, snaps_ref, step):
    rank_width, tile = basis_ref.shape
    snaps = jnp.concatenate([snaps_ref[t] for t in range(snaps_ref.shape[0])], 0)
    cell = step * tile + lax.broadcasted_iota(jnp.int32, snaps.shape, 1)
    snaps = jnp.where(cell < counts_ref[0] * BLOCK, snaps, 0.0)
    return jnp.concatenate([basis_ref[...], snaps], 0)


def gram_kernel(counts_ref, basis_ref, snaps_ref, out_ref, main, cross):
    step = pl.program_id(0)
    rank_width = basis_ref.shape[0]

    @pl.when(step == 0)
    def _():
        main[...] = jnp.zeros_like(main)
        cross[...] = jnp.zeros_like(cross)

    high, low = split_two(masked_stack(counts_ref, basis_ref, snaps_ref, step))
    dims = ((1,), (1,))
    main[...] += dot_half(high, high, dims) + dot_half(low, low, dims)
    cross[...] += dot_half(high, low, dims)

    @pl.when(step == pl.num_programs(0) - 1)
    def _():
        total = main[...] + cross[...] + cross[...].T
        parts = total.shape[0] // rank_width
        row = 0
        for i in range(parts):
            for j in range(i + 1):
                block = total[
                    i * rank_width : (i + 1) * rank_width, j * rank_width : (j + 1) * rank_width
                ]
                if i == 0:
                    spot = (lax.broadcasted_iota(jnp.int32, block.shape, 0) == 0) & (
                        lax.broadcasted_iota(jnp.int32, block.shape, 1) == rank_width - 1
                    )
                    block = jnp.where(spot, counts_ref[0].astype(F32), block)
                out_ref[row : row + rank_width, :] = block
                row += rank_width
        if row < out_ref.shape[0]:
            out_ref[row:, :] = jnp.zeros((out_ref.shape[0] - row, out_ref.shape[1]), F32)


def sum_kernel(
    groups, near, far, in_ref, out_ref, near_buf, far_buf, all_buf,
    near_send, near_recv, far_send, far_recv, back_send, back_recv,
):
    grp, dev = lax.axis_index("grp"), lax.axis_index("dev")
    level, across = dev // near, lax.rem(dev, near)
    members = groups * near
    me = grp * near + across
    chunk = in_ref.shape[0] // members

    def member(offset):
        rank = lax.rem(me + offset, members)
        return rank, (rank // near, level * near + lax.rem(rank, near))

    def along(offset):
        return (grp, lax.rem(level + offset, far) * near + across)

    barrier = pltpu.get_barrier_semaphore()
    for offset in range(1, members):
        pl.semaphore_signal(barrier, inc=1, device_id=member(offset)[1], device_id_type=MESH)
    for offset in range(1, far):
        pl.semaphore_signal(barrier, inc=1, device_id=along(offset), device_id_type=MESH)
    pl.semaphore_wait(barrier, members - 1 + far - 1)

    copies = []
    for offset in range(1, members):
        rank, where = member(offset)
        copies.append(
            pltpu.make_async_remote_copy(
                src_ref=in_ref.at[pl.ds(pl.multiple_of(rank * chunk, SUB), chunk)],
                dst_ref=near_buf.at[offset],
                send_sem=near_send.at[offset],
                recv_sem=near_recv.at[offset],
                device_id=where,
                device_id_type=MESH,
            )
        )
        copies[-1].start()
    mine = pl.ds(pl.multiple_of(me * chunk, SUB), chunk)
    total = in_ref[mine, :]
    for offset, copy in enumerate(copies, 1):
        copy.wait_recv()
        total = total + near_buf[offset]
    far_buf[level] = total
    sends = copies

    copies = []
    for offset in range(1, far):
        copies.append(
            pltpu.make_async_remote_copy(
                src_ref=far_buf.at[level],
                dst_ref=far_buf.at[level],
                send_sem=far_send.at[offset],
                recv_sem=far_recv.at[offset],
                device_id=along(offset),
                device_id_type=MESH,
            )
        )
        copies[-1].start()
    for copy in copies:
        copy.wait_recv()
    sends = sends + copies
    total = far_buf[0]
    for other in range(1, far):
        total = total + far_buf[other]
    all_buf[mine, :] = total

    copies = []
    for offset in range(1, members):
        copies.append(
            pltpu.make_async_remote_copy(
                src_ref=all_buf.at[mine],
                dst_ref=all_buf.at[mine],
                send_sem=back_send.at[offset],
                recv_sem=back_recv.at[offset],
                device_id=member(offset)[1],
                device_id_type=MESH,
            )
        )
        copies[-1].start()
    for copy in copies:
        copy.wait_recv()
    for copy in sends + copies:
        copy.wait_send()
    out_ref[...] = all_buf[...]


def eliminate(panel, start):
    diagonal, arrays = panel
    halves = PANEL // SUB
    lanes = diagonal.shape[1]
    cols = [
        {
            h: jnp.broadcast_to(diagonal[h * SUB : (h + 1) * SUB, start + j : start + j + 1], (SUB, lanes))
            for h in range(j // SUB, halves)
        }
        for j in range(PANEL)
    ]
    work = [[a[h * SUB : (h + 1) * SUB, :] for h in range(halves)] for a in arrays]
    row = lax.broadcasted_iota(jnp.int32, (SUB, lanes), 0)
    pivots = [jnp.ones((SUB, lanes), F32) for _ in range(halves)]
    for j in range(PANEL):
        half, sub = j // SUB, j % SUB
        pivot = jnp.broadcast_to(cols[j][half][sub : sub + 1, :], (SUB, lanes))
        pivots[half] = jnp.where(row == sub, pivot, pivots[half])
        guess = pl.reciprocal(pivot, approx=True)
        fix = 2.0 - pivot * guess
        scaled = {h: (cols[j][h] * guess) * fix for h in range(half, halves)}
        for k in range(j + 1, PANEL):
            lead = jnp.broadcast_to(cols[j][k // SUB][k % SUB : k % SUB + 1, :], (SUB, lanes))
            for h in range(k // SUB, halves):
                cols[k][h] = cols[k][h] - scaled[h] * lead
        below = {**scaled, half: jnp.where(row > sub, scaled[half], 0.0)}
        for target in work:
            lead = jnp.broadcast_to(target[half][sub : sub + 1, :], (SUB, lanes))
            for h in range(half, halves):
                target[h] = target[h] - below[h] * lead
    out = []
    scales = []
    for h in range(halves):
        guess = lax.rsqrt(pivots[h])
        scales.append(guess * (1.5 - 0.5 * pivots[h] * guess * guess))
    for target in work:
        out.append(jnp.concatenate([target[h] * scales[h] for h in range(halves)], 0))
    return out


def outer_rows(rows, first):
    high, mid, low = split_three(rows)
    left = jnp.concatenate([high, high, mid, high, mid, low], 0)
    right = jnp.concatenate([high, mid, high, low, mid, high], 0)
    return dot_half(left, right, ((0,), (0,)))[first:, :]


def lower_inverse(ref, size):
    for start in range(0, size, PANEL):
        stop = start + PANEL
        rows = ref[start:stop, :]
        lane = lax.broadcasted_iota(jnp.int32, rows.shape, 1)
        sub = lax.broadcasted_iota(jnp.int32, rows.shape, 0)
        inside = (lane >= start) & (lane < stop)
        eye = (lane == sub + start).astype(F32)
        (rows,) = eliminate((rows, [jnp.where(inside, eye, rows)]), start)
        ref[start:stop, :] = rows
        if stop < size:
            rest = ref[stop:, :]
            lane = lax.broadcasted_iota(jnp.int32, rest.shape, 1)
            rest = jnp.where((lane >= start) & (lane < stop), 0.0, rest)
            masked = rows
            ref[stop:, :] = rest - outer_rows(masked, stop)[: size - stop, :]


def factor_and_inverse(ref, size):
    for start in range(0, size, PANEL):
        stop = start + PANEL
        rows = ref[start:stop, :]
        (rows,) = eliminate((rows, [rows]), start)
        ref[start:stop, :] = rows
        if stop < size:
            ref[stop:, :] = ref[stop:, :] - outer_rows(rows, stop)[: size - stop, :]


def core_kernel(
    batch, updates, counts_ref, sum_ref, values_ref, basis_hbm, snaps_hbm, out_hbm, new_values_ref,
    gram, core, square, frame, big, small, coeff_ref, stack, result, basis_sem, snaps_sem, out_sem,
):
    rank = values_ref.shape[1]
    tiles, _, tile = stack.shape

    def tile_copies(i):
        spot = pl.ds(pl.multiple_of(i * tile, tile), tile)
        return [
            pltpu.make_async_copy(
                basis_hbm.at[:, spot], stack.at[i, pl.ds(0, rank)], basis_sem.at[i]
            )
        ] + [
            pltpu.make_async_copy(
                snaps_hbm.at[t, :, spot],
                stack.at[i, pl.ds(rank + t * batch, batch)],
                snaps_sem.at[t, i],
            )
            for t in range(updates)
        ]

    def out_copy(i):
        spot = pl.ds(pl.multiple_of(i * tile, tile), tile)
        return pltpu.make_async_copy(result.at[i], out_hbm.at[:, spot], out_sem.at[i])

    def fetch(i, carry):
        for copy in tile_copies(i):
            copy.start()
        return carry

    lax.fori_loop(0, tiles, fetch, 0)
    width = gram.shape[0]
    rows = lax.broadcasted_iota(jnp.int32, (rank, rank), 0)
    lanes = lax.broadcasted_iota(jnp.int32, (rank, rank), 1)
    eye = rows == lanes
    count = sum_ref[0:1, rank - 1 : rank]
    wet_total = count * BLOCK
    parts = width // rank
    row = 0
    for i in range(parts):
        for j in range(i + 1):
            block = sum_ref[row : row + rank, :]
            row += rank
            if i == 0:
                block = jnp.where((rows == 0) & (lanes == rank - 1), block.T, block)
            gram[i * rank : (i + 1) * rank, j * rank : (j + 1) * rank] = block
            if i != j:
                gram[j * rank : (j + 1) * rank, i * rank : (i + 1) * rank] = block.T

    wide_rows = lax.broadcasted_iota(jnp.int32, (rank, width), 0)
    wide_lanes = lax.broadcasted_iota(jnp.int32, (rank, width), 1)
    start_frame = (wide_rows == wide_lanes).astype(F32)
    coeff_ref[...] = start_frame
    core[...] = jnp.zeros_like(core)
    diag = jnp.where(eye, values_ref[...], 0.0)

    batch_rows = lax.broadcasted_iota(jnp.int32, (batch, width), 0)
    batch_lanes = lax.broadcasted_iota(jnp.int32, (batch, width), 1)
    small_rows = lax.broadcasted_iota(jnp.int32, (batch, batch), 0)
    small_lanes = lax.broadcasted_iota(jnp.int32, (batch, batch), 1)

    for index in range(updates):
        coeff = coeff_ref[...]
        first = rank + index * batch
        projected = gram[:rank, :] if index == 0 else nn(coeff, gram[...])
        project = projected[:, first : first + batch] / wet_total
        picker = (batch_lanes == first + batch_rows).astype(F32)
        if index == 0:
            remain = picker - jnp.concatenate(
                [project.T, jnp.zeros((batch, width - rank), F32)], 1
            )
        else:
            remain = picker - tn(project, coeff)
        small[:, :batch] = nt(nn(remain, gram[...]), remain) / wet_total
        small[:, batch:] = (small_rows == small_lanes).astype(F32)
        factor_and_inverse(small, batch)
        factor_t = jnp.where(small_lanes >= small_rows, small[:, :batch], 0.0)
        fresh = nn(small[:, batch:], remain)
        core[:rank, :rank] = diag
        core[:rank, rank : rank + batch] = project
        core[rank : rank + batch, rank : rank + batch] = factor_t
        square[...] = nt(core[...], core[...])

        def sweep(step, carry):
            @pl.when(step == 0)
            def _():
                frame[...] = square[:rank, :]

            @pl.when(step > 0)
            def _():
                frame[...] = nn(frame[...], square[...])

            grown = frame[...]
            big[...] = nt(grown, grown)
            lower_inverse(big, rank)
            inverse = jnp.where(lanes <= rows, big[...], 0.0)
            frame[...] = nn(inverse, grown)
            return carry

        lax.fori_loop(0, SWEEPS, sweep, 0)
        frame_now = frame[...]
        rotated = nn(frame_now, core[...])
        lengths = jnp.sqrt(jnp.sum(rotated * rotated, axis=1, keepdims=True))
        diag = jnp.where(eye, lengths, 0.0)
        if index == 0:
            carried = jnp.concatenate(
                [frame_now[:, :rank], jnp.zeros((rank, width - rank), F32)], 1
            )
        else:
            carried = nn(frame_now[:, :rank], coeff)
        coeff_ref[...] = carried + nn(frame_now[:, rank : rank + batch], fresh)
    new_values_ref[...] = jnp.sum(diag, axis=0, keepdims=True)

    coeff_high, coeff_low = split_two(coeff_ref[...])
    coeff_both = jnp.concatenate([coeff_high, coeff_low], 0)
    dims = ((1,), (0,))

    def apply(i, carry):
        for copy in tile_copies(i):
            copy.wait()
        cell = i * tile + lax.broadcasted_iota(jnp.int32, (width - rank, tile), 1)
        snaps = jnp.where(cell < counts_ref[0] * BLOCK, stack[i, rank:, :], 0.0)
        high, low = split_two(jnp.concatenate([stack[i, :rank, :], snaps], 0))
        both = dot_half(coeff_both, high, dims)
        result[i] = both[:rank, :] + (both[rank:, :] + dot_half(coeff_high, low, dims))
        out_copy(i).start()
        return carry

    lax.fori_loop(0, tiles, apply, 0)

    def drain(i, carry):
        out_copy(i).wait()
        return carry

    lax.fori_loop(0, tiles, drain, 0)


def per_device(groups, devs, basis_old, values_old, snapshots, wet_counts):
    rank, cells = basis_old.shape
    updates, batch = snapshots.shape[0], snapshots.shape[1]
    width = rank + updates * batch
    near = 1
    while (2 * near) * (2 * near) <= devs and devs % (2 * near) == 0:
        near *= 2
    far = devs // near
    members = groups * near
    parts = width // rank
    rows = rank * parts * (parts + 1) // 2
    chunk = -(-rows // (members * SUB)) * SUB
    padded = chunk * members
    tile = min(TILE, cells)

    in_specs = [
        pl.BlockSpec(memory_space=pltpu.SMEM),
        pl.BlockSpec((rank, tile), lambda i: (0, i)),
        pl.BlockSpec((updates, batch, tile), lambda i: (0, 0, i)),
    ]
    vmem = pl.BlockSpec(memory_space=pltpu.VMEM)
    local = pl.pallas_call(
        gram_kernel,
        grid=(cells // tile,),
        out_shape=jax.ShapeDtypeStruct((padded, rank), F32),
        in_specs=in_specs,
        out_specs=pl.BlockSpec((padded, rank), lambda i: (0, 0)),
        scratch_shapes=[pltpu.VMEM((width, width), F32)] * 2,
        compiler_params=pltpu.CompilerParams(vmem_limit_bytes=48 << 20),
    )(wet_counts, basis_old, snapshots)

    summed = pl.pallas_call(
        functools.partial(sum_kernel, groups, near, far),
        out_shape=jax.ShapeDtypeStruct((padded, rank), F32),
        in_specs=[vmem],
        out_specs=vmem,
        scratch_shapes=[
            pltpu.VMEM((members, chunk, rank), F32),
            pltpu.VMEM((far, chunk, rank), F32),
            pltpu.VMEM((padded, rank), F32),
            pltpu.SemaphoreType.DMA((members,)),
            pltpu.SemaphoreType.DMA((members,)),
            pltpu.SemaphoreType.DMA((far,)),
            pltpu.SemaphoreType.DMA((far,)),
            pltpu.SemaphoreType.DMA((members,)),
            pltpu.SemaphoreType.DMA((members,)),
        ],
        compiler_params=pltpu.CompilerParams(collective_id=0, has_side_effects=True),
    )(local)

    tiles = cells // tile
    hbm = pl.BlockSpec(memory_space=pl.ANY)
    basis_new, values = pl.pallas_call(
        functools.partial(core_kernel, batch, updates),
        out_shape=(
            jax.ShapeDtypeStruct((rank, cells), F32),
            jax.ShapeDtypeStruct((1, rank), F32),
        ),
        in_specs=[in_specs[0], vmem, vmem, hbm, hbm],
        out_specs=(hbm, vmem),
        scratch_shapes=[
            pltpu.VMEM((width, width), F32),
            pltpu.VMEM((width, width), F32),
            pltpu.VMEM((width, width), F32),
            pltpu.VMEM((rank, width), F32),
            pltpu.VMEM((rank, rank), F32),
            pltpu.VMEM((batch, 2 * batch), F32),
            pltpu.VMEM((rank, width), F32),
            pltpu.VMEM((tiles, width, tile), F32),
            pltpu.VMEM((tiles, rank, tile), F32),
            pltpu.SemaphoreType.DMA((tiles,)),
            pltpu.SemaphoreType.DMA((updates, tiles)),
            pltpu.SemaphoreType.DMA((tiles,)),
        ],
        compiler_params=pltpu.CompilerParams(vmem_limit_bytes=52 << 20),
    )(wet_counts, summed, values_old.reshape(1, rank), basis_old, snapshots)
    return basis_new, values.reshape(rank)


def solution(mesh):
    return jax.shard_map(
        functools.partial(per_device, mesh.shape["grp"], mesh.shape["dev"]),
        mesh=mesh,
        in_specs=(P(None, ("grp", "dev")), P(), P(None, None, ("grp", "dev")), P(("grp", "dev"))),
        out_specs=(P(None, ("grp", "dev")), P()),
        check_vma=False,
    )
```

```python
import functools

import jax
import jax.numpy as jnp
from jax import lax
from jax.experimental import pallas as pl
from jax.experimental.pallas import tpu as pltpu
from jax.sharding import PartitionSpec as P

BLOCK = 128
SWEEPS = 3
PANEL = 32
SUB = 8
TILE = 1024
MESH = pl.DeviceIdType.MESH
F32 = jnp.float32
BF16 = jnp.bfloat16


def dot_full(left_op, right_op, dims):
    return lax.dot_general(
        left_op, right_op, (dims, ((), ())), precision=lax.Precision.HIGHEST, preferred_element_type=F32
    )


def nn(left_op, right_op):
    return dot_full(left_op, right_op, ((1,), (0,)))


def nt(left_op, right_op):
    return dot_full(left_op, right_op, ((1,), (1,)))


def tn(left_op, right_op):
    return dot_full(left_op, right_op, ((0,), (0,)))


def dot_half(left_op, right_op, dims):
    return lax.dot_general(left_op, right_op, (dims, ((), ())), preferred_element_type=F32)


def split_two(x):
    high = x.astype(BF16)
    return high, (x - high.astype(F32)).astype(BF16)


def split_three(x):
    high = x.astype(BF16)
    rest = x - high.astype(F32)
    mid = rest.astype(BF16)
    return high, mid, (rest - mid.astype(F32)).astype(BF16)


def stack_copies(basis_hbm, snaps_hbm, stack, basis_sem, snaps_sem, i):
    rank, updates, batch = basis_hbm.shape[0], snaps_hbm.shape[0], snaps_hbm.shape[1]
    tile = stack.shape[2]
    spot = pl.ds(pl.multiple_of(i * tile, tile), tile)
    return [
        pltpu.make_async_copy(basis_hbm.at[:, spot], stack.at[i, pl.ds(0, rank)], basis_sem.at[i])
    ] + [
        pltpu.make_async_copy(
            snaps_hbm.at[t, :, spot],
            stack.at[i, pl.ds(rank + t * batch, batch)],
            snaps_sem.at[t, i],
        )
        for t in range(updates)
    ]


def masked_parts(counts_ref, stack, rank, i):
    snaps = stack[i, rank:, :]
    cell = i * stack.shape[2] + lax.broadcasted_iota(jnp.int32, snaps.shape, 1)
    snaps = jnp.where(cell < counts_ref[0] * BLOCK, snaps, 0.0)
    return split_two(jnp.concatenate([stack[i, :rank, :], snaps], 0))


def pack_gram(total, count, rank, out_ref):
    row = 0
    for i in range(total.shape[0] // rank):
        for j in range(i + 1):
            block = total[i * rank : (i + 1) * rank, j * rank : (j + 1) * rank]
            if i == 0:
                spot = (lax.broadcasted_iota(jnp.int32, block.shape, 0) == 0) & (
                    lax.broadcasted_iota(jnp.int32, block.shape, 1) == rank - 1
                )
                block = jnp.where(spot, count, block)
            out_ref[row : row + rank, :] = block
            row += rank
    if row < out_ref.shape[0]:
        out_ref[row:, :] = jnp.zeros((out_ref.shape[0] - row, out_ref.shape[1]), F32)


def gram_kernel(
    groups, near, far, counts_ref, basis_hbm, snaps_hbm, out_ref,
    stack, main, cross, in_ref, near_buf, far_buf, all_buf, basis_sem, snaps_sem,
    near_send, near_recv, far_send, far_recv, back_send, back_recv,
):
    grp, dev = lax.axis_index("grp"), lax.axis_index("dev")
    level, across = dev // near, lax.rem(dev, near)
    members = groups * near
    me = grp * near + across
    chunk = in_ref.shape[0] // members

    def member(offset):
        rank = lax.rem(me + offset, members)
        return rank, (rank // near, level * near + lax.rem(rank, near))

    def along(offset):
        return (grp, lax.rem(level + offset, far) * near + across)

    barrier = pltpu.get_barrier_semaphore()
    for offset in range(1, members):
        pl.semaphore_signal(barrier, inc=1, device_id=member(offset)[1], device_id_type=MESH)
    for offset in range(1, far):
        pl.semaphore_signal(barrier, inc=1, device_id=along(offset), device_id_type=MESH)

    tiles = stack.shape[0]
    rank_width = basis_hbm.shape[0]

    def fetch(i, carry):
        for copy in stack_copies(basis_hbm, snaps_hbm, stack, basis_sem, snaps_sem, i):
            copy.start()
        return carry

    lax.fori_loop(0, tiles, fetch, 0)
    main[...] = jnp.zeros_like(main)
    cross[...] = jnp.zeros_like(cross)

    def accumulate(i, carry):
        for copy in stack_copies(basis_hbm, snaps_hbm, stack, basis_sem, snaps_sem, i):
            copy.wait()
        high, low = masked_parts(counts_ref, stack, rank_width, i)
        dims = ((1,), (1,))
        main[...] += dot_half(high, high, dims) + dot_half(low, low, dims)
        cross[...] += dot_half(high, low, dims)
        return carry

    lax.fori_loop(0, tiles, accumulate, 0)
    total = main[...] + cross[...] + cross[...].T
    pack_gram(total, counts_ref[0].astype(F32), rank_width, in_ref)
    pl.semaphore_wait(barrier, members - 1 + far - 1)

    copies = []
    for offset in range(1, members):
        rank, where = member(offset)
        copies.append(
            pltpu.make_async_remote_copy(
                src_ref=in_ref.at[pl.ds(pl.multiple_of(rank * chunk, SUB), chunk)],
                dst_ref=near_buf.at[offset],
                send_sem=near_send.at[offset],
                recv_sem=near_recv.at[offset],
                device_id=where,
                device_id_type=MESH,
            )
        )
        copies[-1].start()
    mine = pl.ds(pl.multiple_of(me * chunk, SUB), chunk)
    total = in_ref[mine, :]
    for offset, copy in enumerate(copies, 1):
        copy.wait_recv()
        total = total + near_buf[offset]
    far_buf[level] = total
    sends = copies

    copies = []
    for offset in range(1, far):
        copies.append(
            pltpu.make_async_remote_copy(
                src_ref=far_buf.at[level],
                dst_ref=far_buf.at[level],
                send_sem=far_send.at[offset],
                recv_sem=far_recv.at[offset],
                device_id=along(offset),
                device_id_type=MESH,
            )
        )
        copies[-1].start()
    for copy in copies:
        copy.wait_recv()
    sends = sends + copies
    total = far_buf[0]
    for other in range(1, far):
        total = total + far_buf[other]
    all_buf[mine, :] = total

    copies = []
    for offset in range(1, members):
        copies.append(
            pltpu.make_async_remote_copy(
                src_ref=all_buf.at[mine],
                dst_ref=all_buf.at[mine],
                send_sem=back_send.at[offset],
                recv_sem=back_recv.at[offset],
                device_id=member(offset)[1],
                device_id_type=MESH,
            )
        )
        copies[-1].start()
    for copy in copies:
        copy.wait_recv()
    for copy in sends + copies:
        copy.wait_send()
    out_ref[...] = all_buf[...]


def eliminate(panel, start):
    diagonal, arrays = panel
    halves = PANEL // SUB
    lanes = diagonal.shape[1]
    cols = [
        {
            h: jnp.broadcast_to(diagonal[h * SUB : (h + 1) * SUB, start + j : start + j + 1], (SUB, lanes))
            for h in range(j // SUB, halves)
        }
        for j in range(PANEL)
    ]
    work = [[a[h * SUB : (h + 1) * SUB, :] for h in range(halves)] for a in arrays]
    row = lax.broadcasted_iota(jnp.int32, (SUB, lanes), 0)
    pivots = [jnp.ones((SUB, lanes), F32) for _ in range(halves)]
    pivot = jnp.broadcast_to(cols[0][0][0:1, :], (SUB, lanes))
    for j in range(PANEL):
        half, sub = j // SUB, j % SUB
        pivots[half] = jnp.where(row == sub, pivot, pivots[half])
        guess = pl.reciprocal(pivot, approx=True)
        fix = 2.0 - pivot * guess
        if j + 1 < PANEL:
            ahead, spot = (j + 1) // SUB, (j + 1) % SUB
            lead = jnp.broadcast_to(cols[j][ahead][spot : spot + 1, :], (SUB, lanes))
            pivot = jnp.broadcast_to(cols[j + 1][ahead][spot : spot + 1, :], (SUB, lanes))
            pivot = pivot - ((lead * guess) * lead) * fix
        scaled = {h: (cols[j][h] * guess) * fix for h in range(half, halves)}
        for k in range(j + 1, PANEL):
            lead = jnp.broadcast_to(cols[j][k // SUB][k % SUB : k % SUB + 1, :], (SUB, lanes))
            for h in range(k // SUB, halves):
                cols[k][h] = cols[k][h] - scaled[h] * lead
        below = {**scaled, half: jnp.where(row > sub, scaled[half], 0.0)}
        for target in work:
            lead = jnp.broadcast_to(target[half][sub : sub + 1, :], (SUB, lanes))
            for h in range(half, halves):
                target[h] = target[h] - below[h] * lead
    out = []
    scales = []
    for h in range(halves):
        guess = lax.rsqrt(pivots[h])
        scales.append(guess * (1.5 - 0.5 * pivots[h] * guess * guess))
    for target in work:
        out.append(jnp.concatenate([target[h] * scales[h] for h in range(halves)], 0))
    return out


def outer_rows(rows, first):
    high, mid, low = split_three(rows)
    left = jnp.concatenate([high, high, mid, high, mid, low], 0)
    right = jnp.concatenate([high, mid, high, low, mid, high], 0)
    return dot_half(left, right, ((0,), (0,)))[first:, :]


def lower_inverse(ref, size):
    for start in range(0, size, PANEL):
        stop = start + PANEL
        rows = ref[start:stop, :]
        lane = lax.broadcasted_iota(jnp.int32, rows.shape, 1)
        sub = lax.broadcasted_iota(jnp.int32, rows.shape, 0)
        inside = (lane >= start) & (lane < stop)
        eye = (lane == sub + start).astype(F32)
        (rows,) = eliminate((rows, [jnp.where(inside, eye, rows)]), start)
        ref[start:stop, :] = rows
        if stop < size:
            rest = ref[stop:, :]
            lane = lax.broadcasted_iota(jnp.int32, rest.shape, 1)
            rest = jnp.where((lane >= start) & (lane < stop), 0.0, rest)
            masked = rows
            ref[stop:, :] = rest - outer_rows(masked, stop)[: size - stop, :]


def factor_and_inverse(ref, size):
    for start in range(0, size, PANEL):
        stop = start + PANEL
        rows = ref[start:stop, :]
        (rows,) = eliminate((rows, [rows]), start)
        ref[start:stop, :] = rows
        if stop < size:
            ref[stop:, :] = ref[stop:, :] - outer_rows(rows, stop)[: size - stop, :]


def core_kernel(
    batch, updates, counts_ref, sum_ref, values_ref, basis_hbm, snaps_hbm, out_hbm, new_values_ref,
    gram, core, square, frame, big, small, coeff_ref, stack, result, basis_sem, snaps_sem, out_sem,
):
    rank = values_ref.shape[1]
    tiles, _, tile = stack.shape

    def tile_copies(i):
        return stack_copies(basis_hbm, snaps_hbm, stack, basis_sem, snaps_sem, i)

    def out_copy(i):
        spot = pl.ds(pl.multiple_of(i * tile, tile), tile)
        return pltpu.make_async_copy(result.at[i], out_hbm.at[:, spot], out_sem.at[i])

    def fetch(i, carry):
        for copy in tile_copies(i):
            copy.start()
        return carry

    lax.fori_loop(0, tiles, fetch, 0)
    width = gram.shape[0]
    rows = lax.broadcasted_iota(jnp.int32, (rank, rank), 0)
    lanes = lax.broadcasted_iota(jnp.int32, (rank, rank), 1)
    eye = rows == lanes
    count = sum_ref[0:1, rank - 1 : rank]
    wet_total = count * BLOCK
    parts = width // rank
    row = 0
    for i in range(parts):
        for j in range(i + 1):
            block = sum_ref[row : row + rank, :]
            row += rank
            if i == 0:
                block = jnp.where((rows == 0) & (lanes == rank - 1), block.T, block)
            gram[i * rank : (i + 1) * rank, j * rank : (j + 1) * rank] = block
            if i != j:
                gram[j * rank : (j + 1) * rank, i * rank : (i + 1) * rank] = block.T

    wide_rows = lax.broadcasted_iota(jnp.int32, (rank, width), 0)
    wide_lanes = lax.broadcasted_iota(jnp.int32, (rank, width), 1)
    start_frame = (wide_rows == wide_lanes).astype(F32)
    coeff_ref[...] = start_frame
    core[...] = jnp.zeros_like(core)
    diag = jnp.where(eye, values_ref[...], 0.0)

    batch_rows = lax.broadcasted_iota(jnp.int32, (batch, width), 0)
    batch_lanes = lax.broadcasted_iota(jnp.int32, (batch, width), 1)
    small_rows = lax.broadcasted_iota(jnp.int32, (batch, batch), 0)
    small_lanes = lax.broadcasted_iota(jnp.int32, (batch, batch), 1)

    for index in range(updates):
        coeff = coeff_ref[...]
        first = rank + index * batch
        projected = gram[:rank, :] if index == 0 else nn(coeff, gram[...])
        project = projected[:, first : first + batch] / wet_total
        picker = (batch_lanes == first + batch_rows).astype(F32)
        if index == 0:
            remain = picker - jnp.concatenate(
                [project.T, jnp.zeros((batch, width - rank), F32)], 1
            )
        else:
            remain = picker - tn(project, coeff)
        small[:, :batch] = nt(nn(remain, gram[...]), remain) / wet_total
        small[:, batch:] = (small_rows == small_lanes).astype(F32)
        factor_and_inverse(small, batch)
        factor_t = jnp.where(small_lanes >= small_rows, small[:, :batch], 0.0)
        fresh = nn(small[:, batch:], remain)
        core[:rank, :rank] = diag
        core[:rank, rank : rank + batch] = project
        core[rank : rank + batch, rank : rank + batch] = factor_t
        square[...] = nt(core[...], core[...])

        def sweep(step, carry):
            @pl.when(step == 0)
            def _():
                frame[...] = square[:rank, :]

            @pl.when(step > 0)
            def _():
                frame[...] = nn(frame[...], square[...])

            grown = frame[...]
            big[...] = nt(grown, grown)
            lower_inverse(big, rank)
            inverse = jnp.where(lanes <= rows, big[...], 0.0)
            frame[...] = nn(inverse, grown)
            return carry

        lax.fori_loop(0, SWEEPS, sweep, 0)
        frame_now = frame[...]
        rotated = nn(frame_now, core[...])
        lengths = jnp.sqrt(jnp.sum(rotated * rotated, axis=1, keepdims=True))
        diag = jnp.where(eye, lengths, 0.0)
        if index == 0:
            carried = jnp.concatenate(
                [frame_now[:, :rank], jnp.zeros((rank, width - rank), F32)], 1
            )
        else:
            carried = nn(frame_now[:, :rank], coeff)
        coeff_ref[...] = carried + nn(frame_now[:, rank : rank + batch], fresh)
    new_values_ref[...] = jnp.sum(diag, axis=0, keepdims=True)

    coeff_high, coeff_low = split_two(coeff_ref[...])
    coeff_both = jnp.concatenate([coeff_high, coeff_low], 0)
    dims = ((1,), (0,))

    def apply(i, carry):
        for copy in tile_copies(i):
            copy.wait()
        high, low = masked_parts(counts_ref, stack, rank, i)
        both = dot_half(coeff_both, high, dims)
        result[i] = both[:rank, :] + (both[rank:, :] + dot_half(coeff_high, low, dims))
        out_copy(i).start()
        return carry

    lax.fori_loop(0, tiles, apply, 0)

    def drain(i, carry):
        out_copy(i).wait()
        return carry

    lax.fori_loop(0, tiles, drain, 0)


def per_device(groups, devs, basis_old, values_old, snapshots, wet_counts):
    rank, cells = basis_old.shape
    updates, batch = snapshots.shape[0], snapshots.shape[1]
    width = rank + updates * batch
    near = 1
    while (2 * near) * (2 * near) <= devs and devs % (2 * near) == 0:
        near *= 2
    far = devs // near
    members = groups * near
    parts = width // rank
    rows = rank * parts * (parts + 1) // 2
    chunk = -(-rows // (members * SUB)) * SUB
    padded = chunk * members
    tile = min(TILE, cells)

    tiles = cells // tile
    smem = pl.BlockSpec(memory_space=pltpu.SMEM)
    vmem = pl.BlockSpec(memory_space=pltpu.VMEM)
    hbm = pl.BlockSpec(memory_space=pl.ANY)
    summed = pl.pallas_call(
        functools.partial(gram_kernel, groups, near, far),
        out_shape=jax.ShapeDtypeStruct((padded, rank), F32),
        in_specs=[smem, hbm, hbm],
        out_specs=vmem,
        scratch_shapes=[
            pltpu.VMEM((tiles, width, tile), F32),
            pltpu.VMEM((width, width), F32),
            pltpu.VMEM((width, width), F32),
            pltpu.VMEM((padded, rank), F32),
            pltpu.VMEM((members, chunk, rank), F32),
            pltpu.VMEM((far, chunk, rank), F32),
            pltpu.VMEM((padded, rank), F32),
            pltpu.SemaphoreType.DMA((tiles,)),
            pltpu.SemaphoreType.DMA((updates, tiles)),
            pltpu.SemaphoreType.DMA((members,)),
            pltpu.SemaphoreType.DMA((members,)),
            pltpu.SemaphoreType.DMA((far,)),
            pltpu.SemaphoreType.DMA((far,)),
            pltpu.SemaphoreType.DMA((members,)),
            pltpu.SemaphoreType.DMA((members,)),
        ],
        compiler_params=pltpu.CompilerParams(
            collective_id=0, has_side_effects=True, vmem_limit_bytes=52 << 20
        ),
    )(wet_counts, basis_old, snapshots)

    basis_new, values = pl.pallas_call(
        functools.partial(core_kernel, batch, updates),
        out_shape=(
            jax.ShapeDtypeStruct((rank, cells), F32),
            jax.ShapeDtypeStruct((1, rank), F32),
        ),
        in_specs=[smem, vmem, vmem, hbm, hbm],
        out_specs=(hbm, vmem),
        scratch_shapes=[
            pltpu.VMEM((width, width), F32),
            pltpu.VMEM((width, width), F32),
            pltpu.VMEM((width, width), F32),
            pltpu.VMEM((rank, width), F32),
            pltpu.VMEM((rank, rank), F32),
            pltpu.VMEM((batch, 2 * batch), F32),
            pltpu.VMEM((rank, width), F32),
            pltpu.VMEM((tiles, width, tile), F32),
            pltpu.VMEM((tiles, rank, tile), F32),
            pltpu.SemaphoreType.DMA((tiles,)),
            pltpu.SemaphoreType.DMA((updates, tiles)),
            pltpu.SemaphoreType.DMA((tiles,)),
        ],
        compiler_params=pltpu.CompilerParams(vmem_limit_bytes=52 << 20),
    )(wet_counts, summed, values_old.reshape(1, rank), basis_old, snapshots)
    return basis_new, values.reshape(rank)


def solution(mesh):
    return jax.shard_map(
        functools.partial(per_device, mesh.shape["grp"], mesh.shape["dev"]),
        mesh=mesh,
        in_specs=(P(None, ("grp", "dev")), P(), P(None, None, ("grp", "dev")), P(("grp", "dev"))),
        out_specs=(P(None, ("grp", "dev")), P()),
        check_vma=False,
    )
```

```python
import functools

import jax
import jax.numpy as jnp
from jax import lax
from jax.experimental import pallas as pl
from jax.experimental.pallas import tpu as pltpu
from jax.sharding import PartitionSpec as P

BLOCK = 128
SWEEPS = 3
PANEL = 32
SUB = 8
TILE = 2048
MESH = pl.DeviceIdType.MESH
F32 = jnp.float32
BF16 = jnp.bfloat16


def dot_half(left_op, right_op, dims):
    return lax.dot_general(left_op, right_op, (dims, ((), ())), preferred_element_type=F32)


def split_two(x):
    high = x.astype(BF16)
    return high, (x - high.astype(F32)).astype(BF16)


def split_three(x):
    high = x.astype(BF16)
    rest = x - high.astype(F32)
    mid = rest.astype(BF16)
    return high, mid, (rest - mid.astype(F32)).astype(BF16)


def dot_full(left_op, right_op, dims):
    left_axis = 1 - dims[0][0]
    rows = left_op.shape[left_axis]
    left_terms, right_terms = split_three(left_op), split_three(right_op)
    total = None
    for place in (2, 1, 0):
        used = 3 - place
        stacked = jnp.concatenate(left_terms[:used], left_axis)
        product = dot_half(stacked, right_terms[place], dims)
        part = product[:rows, :]
        if used > 1:
            small = product[rows : 2 * rows, :]
            if used > 2:
                small = small + product[2 * rows :, :]
            part = part + small
        total = part if total is None else part + total
    return total


def nn(left_op, right_op):
    return dot_full(left_op, right_op, ((1,), (0,)))


def nt(left_op, right_op):
    return dot_full(left_op, right_op, ((1,), (1,)))


def tn(left_op, right_op):
    return dot_full(left_op, right_op, ((0,), (0,)))


def self_nt(op):
    rows = op.shape[0]
    high, mid, low = split_three(op)
    dims = ((1,), (1,))
    product = dot_half(jnp.concatenate([high, mid, low], 0), high, dims)
    cross = product[rows : 2 * rows, :] + product[2 * rows :, :]
    return product[:rows, :] + (cross + cross.T + dot_half(mid, mid, dims))


def stack_copies(basis_hbm, snaps_hbm, stack, basis_sem, snaps_sem, i):
    rank, updates, batch = basis_hbm.shape[0], snaps_hbm.shape[0], snaps_hbm.shape[1]
    tile = stack.shape[2]
    spot = pl.ds(pl.multiple_of(i * tile, tile), tile)
    return [
        pltpu.make_async_copy(basis_hbm.at[:, spot], stack.at[i, pl.ds(0, rank)], basis_sem.at[i])
    ] + [
        pltpu.make_async_copy(
            snaps_hbm.at[t, :, spot],
            stack.at[i, pl.ds(rank + t * batch, batch)],
            snaps_sem.at[t, i],
        )
        for t in range(updates)
    ]


def masked_parts(counts_ref, stack, rank, i):
    snaps = stack[i, rank:, :]
    cell = i * stack.shape[2] + lax.broadcasted_iota(jnp.int32, snaps.shape, 1)
    snaps = jnp.where(cell < counts_ref[0] * BLOCK, snaps, 0.0)
    return split_two(jnp.concatenate([stack[i, :rank, :], snaps], 0))


def pack_gram(total, count, rank, out_ref):
    row = 0
    for i in range(total.shape[0] // rank):
        for j in range(i + 1):
            block = total[i * rank : (i + 1) * rank, j * rank : (j + 1) * rank]
            if i == 0:
                spot = (lax.broadcasted_iota(jnp.int32, block.shape, 0) == 0) & (
                    lax.broadcasted_iota(jnp.int32, block.shape, 1) == rank - 1
                )
                block = jnp.where(spot, count, block)
            out_ref[row : row + rank, :] = block
            row += rank
    if row < out_ref.shape[0]:
        out_ref[row:, :] = jnp.zeros((out_ref.shape[0] - row, out_ref.shape[1]), F32)


def gram_kernel(
    groups, near, far, counts_ref, basis_hbm, snaps_hbm, out_ref,
    stack, main, cross, in_ref, near_buf, far_buf, all_buf, basis_sem, snaps_sem,
    near_send, near_recv, far_send, far_recv, back_send, back_recv,
):
    grp, dev = lax.axis_index("grp"), lax.axis_index("dev")
    level, across = dev // near, lax.rem(dev, near)
    members = groups * near
    me = grp * near + across
    chunk = in_ref.shape[0] // members

    def member(offset):
        rank = lax.rem(me + offset, members)
        return rank, (rank // near, level * near + lax.rem(rank, near))

    def along(offset):
        return (grp, lax.rem(level + offset, far) * near + across)

    barrier = pltpu.get_barrier_semaphore()
    for offset in range(1, members):
        pl.semaphore_signal(barrier, inc=1, device_id=member(offset)[1], device_id_type=MESH)
    for offset in range(1, far):
        pl.semaphore_signal(barrier, inc=1, device_id=along(offset), device_id_type=MESH)

    tiles = stack.shape[0]
    rank_width = basis_hbm.shape[0]

    def fetch(i, carry):
        for copy in stack_copies(basis_hbm, snaps_hbm, stack, basis_sem, snaps_sem, i):
            copy.start()
        return carry

    lax.fori_loop(0, tiles, fetch, 0)
    main[...] = jnp.zeros_like(main)
    cross[...] = jnp.zeros_like(cross)

    def accumulate(i, carry):
        for copy in stack_copies(basis_hbm, snaps_hbm, stack, basis_sem, snaps_sem, i):
            copy.wait()
        high, low = masked_parts(counts_ref, stack, rank_width, i)
        dims = ((1,), (1,))
        main[...] += dot_half(high, high, dims) + dot_half(low, low, dims)
        cross[...] += dot_half(high, low, dims)
        return carry

    lax.fori_loop(0, tiles, accumulate, 0)
    total = main[...] + cross[...] + cross[...].T
    pack_gram(total, counts_ref[0].astype(F32), rank_width, in_ref)
    pl.semaphore_wait(barrier, members - 1 + far - 1)

    copies = []
    for offset in range(1, members):
        rank, where = member(offset)
        copies.append(
            pltpu.make_async_remote_copy(
                src_ref=in_ref.at[pl.ds(pl.multiple_of(rank * chunk, SUB), chunk)],
                dst_ref=near_buf.at[offset],
                send_sem=near_send.at[offset],
                recv_sem=near_recv.at[offset],
                device_id=where,
                device_id_type=MESH,
            )
        )
        copies[-1].start()
    mine = pl.ds(pl.multiple_of(me * chunk, SUB), chunk)
    total = in_ref[mine, :]
    for offset, copy in enumerate(copies, 1):
        copy.wait_recv()
        total = total + near_buf[offset]
    far_buf[level] = total
    sends = copies

    copies = []
    for offset in range(1, far):
        copies.append(
            pltpu.make_async_remote_copy(
                src_ref=far_buf.at[level],
                dst_ref=far_buf.at[level],
                send_sem=far_send.at[offset],
                recv_sem=far_recv.at[offset],
                device_id=along(offset),
                device_id_type=MESH,
            )
        )
        copies[-1].start()
    for copy in copies:
        copy.wait_recv()
    sends = sends + copies
    total = far_buf[0]
    for other in range(1, far):
        total = total + far_buf[other]
    all_buf[mine, :] = total

    copies = []
    for offset in range(1, members):
        copies.append(
            pltpu.make_async_remote_copy(
                src_ref=all_buf.at[mine],
                dst_ref=all_buf.at[mine],
                send_sem=back_send.at[offset],
                recv_sem=back_recv.at[offset],
                device_id=member(offset)[1],
                device_id_type=MESH,
            )
        )
        copies[-1].start()
    for copy in copies:
        copy.wait_recv()
    for copy in sends + copies:
        copy.wait_send()
    out_ref[...] = all_buf[...]


def eliminate(panel, start):
    diagonal, arrays = panel
    halves = PANEL // SUB
    lanes = diagonal.shape[1]
    cols = [
        {
            h: jnp.broadcast_to(diagonal[h * SUB : (h + 1) * SUB, start + j : start + j + 1], (SUB, lanes))
            for h in range(j // SUB, halves)
        }
        for j in range(PANEL)
    ]
    work = [[a[h * SUB : (h + 1) * SUB, :] for h in range(halves)] for a in arrays]
    row = lax.broadcasted_iota(jnp.int32, (SUB, lanes), 0)
    pivots = [jnp.ones((SUB, lanes), F32) for _ in range(halves)]
    pivot = jnp.broadcast_to(cols[0][0][0:1, :], (SUB, lanes))
    for j in range(PANEL):
        half, sub = j // SUB, j % SUB
        pivots[half] = jnp.where(row == sub, pivot, pivots[half])
        guess = pl.reciprocal(pivot, approx=True)
        fix = 2.0 - pivot * guess
        if j + 1 < PANEL:
            ahead, spot = (j + 1) // SUB, (j + 1) % SUB
            lead = jnp.broadcast_to(cols[j][ahead][spot : spot + 1, :], (SUB, lanes))
            pivot = jnp.broadcast_to(cols[j + 1][ahead][spot : spot + 1, :], (SUB, lanes))
            pivot = pivot - ((lead * guess) * lead) * fix
        scaled = {h: (cols[j][h] * guess) * fix for h in range(half, halves)}
        for k in range(j + 1, PANEL):
            lead = jnp.broadcast_to(cols[j][k // SUB][k % SUB : k % SUB + 1, :], (SUB, lanes))
            for h in range(k // SUB, halves):
                cols[k][h] = cols[k][h] - scaled[h] * lead
        below = {**scaled, half: jnp.where(row > sub, scaled[half], 0.0)}
        for target in work:
            lead = jnp.broadcast_to(target[half][sub : sub + 1, :], (SUB, lanes))
            for h in range(half, halves):
                target[h] = target[h] - below[h] * lead
    out = []
    scales = []
    for h in range(halves):
        guess = lax.rsqrt(pivots[h])
        scales.append(guess * (1.5 - 0.5 * pivots[h] * guess * guess))
    for target in work:
        out.append(jnp.concatenate([target[h] * scales[h] for h in range(halves)], 0))
    return out


def outer_rows(rows, first):
    high, mid, low = split_three(rows)
    left = jnp.concatenate([high, high, mid, high, mid, low], 0)
    right = jnp.concatenate([high, mid, high, low, mid, high], 0)
    return dot_half(left, right, ((0,), (0,)))[first:, :]


def lower_inverse(ref, size):
    for start in range(0, size, PANEL):
        stop = start + PANEL
        rows = ref[start:stop, :]
        lane = lax.broadcasted_iota(jnp.int32, rows.shape, 1)
        sub = lax.broadcasted_iota(jnp.int32, rows.shape, 0)
        inside = (lane >= start) & (lane < stop)
        eye = (lane == sub + start).astype(F32)
        (rows,) = eliminate((rows, [jnp.where(inside, eye, rows)]), start)
        ref[start:stop, :] = rows
        if stop < size:
            rest = ref[stop:, :]
            lane = lax.broadcasted_iota(jnp.int32, rest.shape, 1)
            rest = jnp.where((lane >= start) & (lane < stop), 0.0, rest)
            masked = rows
            ref[stop:, :] = rest - outer_rows(masked, stop)[: size - stop, :]


def factor_and_inverse(ref, size):
    for start in range(0, size, PANEL):
        stop = start + PANEL
        rows = ref[start:stop, :]
        (rows,) = eliminate((rows, [rows]), start)
        ref[start:stop, :] = rows
        if stop < size:
            ref[stop:, :] = ref[stop:, :] - outer_rows(rows, stop)[: size - stop, :]


def core_kernel(
    batch, updates, counts_ref, sum_ref, values_ref, basis_hbm, snaps_hbm, out_hbm, new_values_ref,
    gram, core, square, frame, big, small, coeff_ref, stack, result, basis_sem, snaps_sem, out_sem,
):
    rank = values_ref.shape[1]
    tiles, _, tile = stack.shape

    def tile_copies(i):
        return stack_copies(basis_hbm, snaps_hbm, stack, basis_sem, snaps_sem, i)

    def out_copy(i):
        spot = pl.ds(pl.multiple_of(i * tile, tile), tile)
        return pltpu.make_async_copy(result.at[i], out_hbm.at[:, spot], out_sem.at[i])

    def fetch(i, carry):
        for copy in tile_copies(i):
            copy.start()
        return carry

    lax.fori_loop(0, tiles, fetch, 0)
    width = gram.shape[0]
    rows = lax.broadcasted_iota(jnp.int32, (rank, rank), 0)
    lanes = lax.broadcasted_iota(jnp.int32, (rank, rank), 1)
    eye = rows == lanes
    count = sum_ref[0:1, rank - 1 : rank]
    wet_total = count * BLOCK
    parts = width // rank
    row = 0
    for i in range(parts):
        for j in range(i + 1):
            block = sum_ref[row : row + rank, :]
            row += rank
            if i == 0:
                block = jnp.where((rows == 0) & (lanes == rank - 1), block.T, block)
            gram[i * rank : (i + 1) * rank, j * rank : (j + 1) * rank] = block
            if i != j:
                gram[j * rank : (j + 1) * rank, i * rank : (i + 1) * rank] = block.T

    wide_rows = lax.broadcasted_iota(jnp.int32, (rank, width), 0)
    wide_lanes = lax.broadcasted_iota(jnp.int32, (rank, width), 1)
    start_frame = (wide_rows == wide_lanes).astype(F32)
    coeff_ref[...] = start_frame
    core[...] = jnp.zeros_like(core)
    diag = jnp.where(eye, values_ref[...], 0.0)

    batch_rows = lax.broadcasted_iota(jnp.int32, (batch, width), 0)
    batch_lanes = lax.broadcasted_iota(jnp.int32, (batch, width), 1)
    small_rows = lax.broadcasted_iota(jnp.int32, (batch, batch), 0)
    small_lanes = lax.broadcasted_iota(jnp.int32, (batch, batch), 1)

    for index in range(updates):
        coeff = coeff_ref[...]
        first = rank + index * batch
        projected = gram[:rank, :] if index == 0 else nn(coeff, gram[...])
        project = projected[:, first : first + batch] / wet_total
        picker = (batch_lanes == first + batch_rows).astype(F32)
        if index == 0:
            remain = picker - jnp.concatenate(
                [project.T, jnp.zeros((batch, width - rank), F32)], 1
            )
        else:
            remain = picker - tn(project, coeff)
        small[:, :batch] = nt(nn(remain, gram[...]), remain) / wet_total
        small[:, batch:] = (small_rows == small_lanes).astype(F32)
        factor_and_inverse(small, batch)
        factor_t = jnp.where(small_lanes >= small_rows, small[:, :batch], 0.0)
        fresh = nn(small[:, batch:], remain)
        core[:rank, :rank] = diag
        core[:rank, rank : rank + batch] = project
        core[rank : rank + batch, rank : rank + batch] = factor_t
        square[...] = self_nt(core[...])

        def sweep(step, carry):
            @pl.when(step == 0)
            def _():
                frame[...] = square[:rank, :]

            @pl.when(step > 0)
            def _():
                frame[...] = nn(frame[...], square[...])

            grown = frame[...]
            big[...] = self_nt(grown)
            lower_inverse(big, rank)
            inverse = jnp.where(lanes <= rows, big[...], 0.0)
            frame[...] = nn(inverse, grown)
            return carry

        lax.fori_loop(0, SWEEPS, sweep, 0)
        frame_now = frame[...]
        rotated = nn(frame_now, core[...])
        lengths = jnp.sqrt(jnp.sum(rotated * rotated, axis=1, keepdims=True))
        diag = jnp.where(eye, lengths, 0.0)
        if index == 0:
            carried = jnp.concatenate(
                [frame_now[:, :rank], jnp.zeros((rank, width - rank), F32)], 1
            )
        else:
            carried = nn(frame_now[:, :rank], coeff)
        coeff_ref[...] = carried + nn(frame_now[:, rank : rank + batch], fresh)
    new_values_ref[...] = jnp.sum(diag, axis=0, keepdims=True)

    coeff_high, coeff_low = split_two(coeff_ref[...])
    coeff_both = jnp.concatenate([coeff_high, coeff_low], 0)
    dims = ((1,), (0,))

    def apply(i, carry):
        for copy in tile_copies(i):
            copy.wait()
        high, low = masked_parts(counts_ref, stack, rank, i)
        both = dot_half(coeff_both, high, dims)
        result[i] = both[:rank, :] + (both[rank:, :] + dot_half(coeff_high, low, dims))
        out_copy(i).start()
        return carry

    lax.fori_loop(0, tiles, apply, 0)

    def drain(i, carry):
        out_copy(i).wait()
        return carry

    lax.fori_loop(0, tiles, drain, 0)


def per_device(groups, devs, basis_old, values_old, snapshots, wet_counts):
    rank, cells = basis_old.shape
    updates, batch = snapshots.shape[0], snapshots.shape[1]
    width = rank + updates * batch
    near = 1
    while (2 * near) * (2 * near) <= devs and devs % (2 * near) == 0:
        near *= 2
    far = devs // near
    members = groups * near
    parts = width // rank
    rows = rank * parts * (parts + 1) // 2
    chunk = -(-rows // (members * SUB)) * SUB
    padded = chunk * members
    tile = min(TILE, cells)

    tiles = cells // tile
    smem = pl.BlockSpec(memory_space=pltpu.SMEM)
    vmem = pl.BlockSpec(memory_space=pltpu.VMEM)
    hbm = pl.BlockSpec(memory_space=pl.ANY)
    summed = pl.pallas_call(
        functools.partial(gram_kernel, groups, near, far),
        out_shape=jax.ShapeDtypeStruct((padded, rank), F32),
        in_specs=[smem, hbm, hbm],
        out_specs=vmem,
        scratch_shapes=[
            pltpu.VMEM((tiles, width, tile), F32),
            pltpu.VMEM((width, width), F32),
            pltpu.VMEM((width, width), F32),
            pltpu.VMEM((padded, rank), F32),
            pltpu.VMEM((members, chunk, rank), F32),
            pltpu.VMEM((far, chunk, rank), F32),
            pltpu.VMEM((padded, rank), F32),
            pltpu.SemaphoreType.DMA((tiles,)),
            pltpu.SemaphoreType.DMA((updates, tiles)),
            pltpu.SemaphoreType.DMA((members,)),
            pltpu.SemaphoreType.DMA((members,)),
            pltpu.SemaphoreType.DMA((far,)),
            pltpu.SemaphoreType.DMA((far,)),
            pltpu.SemaphoreType.DMA((members,)),
            pltpu.SemaphoreType.DMA((members,)),
        ],
        compiler_params=pltpu.CompilerParams(
            collective_id=0, has_side_effects=True, vmem_limit_bytes=52 << 20
        ),
    )(wet_counts, basis_old, snapshots)

    basis_new, values = pl.pallas_call(
        functools.partial(core_kernel, batch, updates),
        out_shape=(
            jax.ShapeDtypeStruct((rank, cells), F32),
            jax.ShapeDtypeStruct((1, rank), F32),
        ),
        in_specs=[smem, vmem, vmem, hbm, hbm],
        out_specs=(hbm, vmem),
        scratch_shapes=[
            pltpu.VMEM((width, width), F32),
            pltpu.VMEM((width, width), F32),
            pltpu.VMEM((width, width), F32),
            pltpu.VMEM((rank, width), F32),
            pltpu.VMEM((rank, rank), F32),
            pltpu.VMEM((batch, 2 * batch), F32),
            pltpu.VMEM((rank, width), F32),
            pltpu.VMEM((tiles, width, tile), F32),
            pltpu.VMEM((tiles, rank, tile), F32),
            pltpu.SemaphoreType.DMA((tiles,)),
            pltpu.SemaphoreType.DMA((updates, tiles)),
            pltpu.SemaphoreType.DMA((tiles,)),
        ],
        compiler_params=pltpu.CompilerParams(vmem_limit_bytes=52 << 20),
    )(wet_counts, summed, values_old.reshape(1, rank), basis_old, snapshots)
    return basis_new, values.reshape(rank)


def solution(mesh):
    return jax.shard_map(
        functools.partial(per_device, mesh.shape["grp"], mesh.shape["dev"]),
        mesh=mesh,
        in_specs=(P(None, ("grp", "dev")), P(), P(None, None, ("grp", "dev")), P(("grp", "dev"))),
        out_specs=(P(None, ("grp", "dev")), P()),
        check_vma=False,
    )
```

```python
import functools

import jax
import jax.numpy as jnp
from jax import lax
from jax.experimental import pallas as pl
from jax.experimental.pallas import tpu as pltpu
from jax.sharding import PartitionSpec as P

BLOCK = 128
SWEEPS = 3
PANEL = 16
SUB = 8
TILE = 2048
MESH = pl.DeviceIdType.MESH
F32 = jnp.float32
BF16 = jnp.bfloat16


def dot_half(left_op, right_op, dims):
    return lax.dot_general(left_op, right_op, (dims, ((), ())), preferred_element_type=F32)


def split_two(x):
    high = x.astype(BF16)
    return high, (x - high.astype(F32)).astype(BF16)


def split_three(x):
    high = x.astype(BF16)
    rest = x - high.astype(F32)
    mid = rest.astype(BF16)
    return high, mid, (rest - mid.astype(F32)).astype(BF16)


def dot_full(left_op, right_op, dims):
    left_axis = 1 - dims[0][0]
    rows = left_op.shape[left_axis]
    left_terms, right_terms = split_three(left_op), split_three(right_op)
    total = None
    for place in (2, 1, 0):
        used = 3 - place
        stacked = jnp.concatenate(left_terms[:used], left_axis)
        product = dot_half(stacked, right_terms[place], dims)
        part = product[:rows, :]
        if used > 1:
            small = product[rows : 2 * rows, :]
            if used > 2:
                small = small + product[2 * rows :, :]
            part = part + small
        total = part if total is None else part + total
    return total


def nn(left_op, right_op):
    return dot_full(left_op, right_op, ((1,), (0,)))


def nt(left_op, right_op):
    return dot_full(left_op, right_op, ((1,), (1,)))


def tn(left_op, right_op):
    return dot_full(left_op, right_op, ((0,), (0,)))


def self_nt(op):
    rows = op.shape[0]
    high, mid, low = split_three(op)
    dims = ((1,), (1,))
    product = dot_half(jnp.concatenate([high, mid, low], 0), high, dims)
    cross = product[rows : 2 * rows, :] + product[2 * rows :, :]
    return product[:rows, :] + (cross + cross.T + dot_half(mid, mid, dims))


def stack_copies(basis_hbm, snaps_hbm, stack, basis_sem, snaps_sem, i):
    rank, updates, batch = basis_hbm.shape[0], snaps_hbm.shape[0], snaps_hbm.shape[1]
    tile = stack.shape[2]
    spot = pl.ds(pl.multiple_of(i * tile, tile), tile)
    return [
        pltpu.make_async_copy(basis_hbm.at[:, spot], stack.at[i, pl.ds(0, rank)], basis_sem.at[i])
    ] + [
        pltpu.make_async_copy(
            snaps_hbm.at[t, :, spot],
            stack.at[i, pl.ds(rank + t * batch, batch)],
            snaps_sem.at[t, i],
        )
        for t in range(updates)
    ]


def masked_parts(counts_ref, stack, rank, i):
    snaps = stack[i, rank:, :]
    cell = i * stack.shape[2] + lax.broadcasted_iota(jnp.int32, snaps.shape, 1)
    snaps = jnp.where(cell < counts_ref[0] * BLOCK, snaps, 0.0)
    return split_two(jnp.concatenate([stack[i, :rank, :], snaps], 0))


def pack_gram(total, count, rank, out_ref):
    row = 0
    for i in range(total.shape[0] // rank):
        for j in range(i + 1):
            block = total[i * rank : (i + 1) * rank, j * rank : (j + 1) * rank]
            if i == 0:
                spot = (lax.broadcasted_iota(jnp.int32, block.shape, 0) == 0) & (
                    lax.broadcasted_iota(jnp.int32, block.shape, 1) == rank - 1
                )
                block = jnp.where(spot, count, block)
            out_ref[row : row + rank, :] = block
            row += rank
    if row < out_ref.shape[0]:
        out_ref[row:, :] = jnp.zeros((out_ref.shape[0] - row, out_ref.shape[1]), F32)


def gram_kernel(
    groups, near, far, counts_ref, basis_hbm, snaps_hbm, out_ref,
    stack, main, cross, in_ref, near_buf, far_buf, all_buf, basis_sem, snaps_sem,
    near_send, near_recv, far_send, far_recv, back_send, back_recv,
):
    grp, dev = lax.axis_index("grp"), lax.axis_index("dev")
    level, across = dev // near, lax.rem(dev, near)
    members = groups * near
    me = grp * near + across
    chunk = in_ref.shape[0] // members

    def member(offset):
        rank = lax.rem(me + offset, members)
        return rank, (rank // near, level * near + lax.rem(rank, near))

    def along(offset):
        return (grp, lax.rem(level + offset, far) * near + across)

    barrier = pltpu.get_barrier_semaphore()
    for offset in range(1, members):
        pl.semaphore_signal(barrier, inc=1, device_id=member(offset)[1], device_id_type=MESH)
    for offset in range(1, far):
        pl.semaphore_signal(barrier, inc=1, device_id=along(offset), device_id_type=MESH)

    tiles = stack.shape[0]
    rank_width = basis_hbm.shape[0]

    def fetch(i, carry):
        for copy in stack_copies(basis_hbm, snaps_hbm, stack, basis_sem, snaps_sem, i):
            copy.start()
        return carry

    lax.fori_loop(0, tiles, fetch, 0)
    main[...] = jnp.zeros_like(main)
    cross[...] = jnp.zeros_like(cross)

    def accumulate(i, carry):
        for copy in stack_copies(basis_hbm, snaps_hbm, stack, basis_sem, snaps_sem, i):
            copy.wait()
        high, low = masked_parts(counts_ref, stack, rank_width, i)
        dims = ((1,), (1,))
        main[...] += dot_half(high, high, dims) + dot_half(low, low, dims)
        cross[...] += dot_half(high, low, dims)
        return carry

    lax.fori_loop(0, tiles, accumulate, 0)
    total = main[...] + cross[...] + cross[...].T
    pack_gram(total, counts_ref[0].astype(F32), rank_width, in_ref)
    pl.semaphore_wait(barrier, members - 1 + far - 1)

    copies = []
    for offset in range(1, members):
        rank, where = member(offset)
        copies.append(
            pltpu.make_async_remote_copy(
                src_ref=in_ref.at[pl.ds(pl.multiple_of(rank * chunk, SUB), chunk)],
                dst_ref=near_buf.at[offset],
                send_sem=near_send.at[offset],
                recv_sem=near_recv.at[offset],
                device_id=where,
                device_id_type=MESH,
            )
        )
        copies[-1].start()
    mine = pl.ds(pl.multiple_of(me * chunk, SUB), chunk)
    total = in_ref[mine, :]
    for offset, copy in enumerate(copies, 1):
        copy.wait_recv()
        total = total + near_buf[offset]
    far_buf[level] = total
    sends = copies

    copies = []
    for offset in range(1, far):
        copies.append(
            pltpu.make_async_remote_copy(
                src_ref=far_buf.at[level],
                dst_ref=far_buf.at[level],
                send_sem=far_send.at[offset],
                recv_sem=far_recv.at[offset],
                device_id=along(offset),
                device_id_type=MESH,
            )
        )
        copies[-1].start()
    for copy in copies:
        copy.wait_recv()
    sends = sends + copies
    total = far_buf[0]
    for other in range(1, far):
        total = total + far_buf[other]
    all_buf[mine, :] = total

    copies = []
    for offset in range(1, members):
        copies.append(
            pltpu.make_async_remote_copy(
                src_ref=all_buf.at[mine],
                dst_ref=all_buf.at[mine],
                send_sem=back_send.at[offset],
                recv_sem=back_recv.at[offset],
                device_id=member(offset)[1],
                device_id_type=MESH,
            )
        )
        copies[-1].start()
    for copy in copies:
        copy.wait_recv()
    for copy in sends + copies:
        copy.wait_send()
    out_ref[...] = all_buf[...]


def eliminate(panel, start):
    diagonal, arrays = panel
    halves = PANEL // SUB
    lanes = diagonal.shape[1]
    cols = [
        {
            h: jnp.broadcast_to(diagonal[h * SUB : (h + 1) * SUB, start + j : start + j + 1], (SUB, lanes))
            for h in range(j // SUB, halves)
        }
        for j in range(PANEL)
    ]
    work = [[a[h * SUB : (h + 1) * SUB, :] for h in range(halves)] for a in arrays]
    row = lax.broadcasted_iota(jnp.int32, (SUB, lanes), 0)
    pivots = [jnp.ones((SUB, lanes), F32) for _ in range(halves)]
    pivot = jnp.broadcast_to(cols[0][0][0:1, :], (SUB, lanes))
    for j in range(PANEL):
        half, sub = j // SUB, j % SUB
        pivots[half] = jnp.where(row == sub, pivot, pivots[half])
        guess = pl.reciprocal(pivot, approx=True)
        fix = 2.0 - pivot * guess
        if j + 1 < PANEL:
            ahead, spot = (j + 1) // SUB, (j + 1) % SUB
            lead = jnp.broadcast_to(cols[j][ahead][spot : spot + 1, :], (SUB, lanes))
            pivot = jnp.broadcast_to(cols[j + 1][ahead][spot : spot + 1, :], (SUB, lanes))
            pivot = pivot - ((lead * guess) * lead) * fix
        scaled = {h: (cols[j][h] * guess) * fix for h in range(half, halves)}
        for k in range(j + 1, PANEL):
            lead = jnp.broadcast_to(cols[j][k // SUB][k % SUB : k % SUB + 1, :], (SUB, lanes))
            for h in range(k // SUB, halves):
                cols[k][h] = cols[k][h] - scaled[h] * lead
        below = {**scaled, half: jnp.where(row > sub, scaled[half], 0.0)}
        for target in work:
            lead = jnp.broadcast_to(target[half][sub : sub + 1, :], (SUB, lanes))
            for h in range(half, halves):
                target[h] = target[h] - below[h] * lead
    out = []
    scales = []
    for h in range(halves):
        guess = lax.rsqrt(pivots[h])
        scales.append(guess * (1.5 - 0.5 * pivots[h] * guess * guess))
    for target in work:
        out.append(jnp.concatenate([target[h] * scales[h] for h in range(halves)], 0))
    return out


def outer_rows(rows, first):
    high, mid, low = split_three(rows)
    left = jnp.concatenate([high, high, mid, high, mid, low], 0)
    right = jnp.concatenate([high, mid, high, low, mid, high], 0)
    return dot_half(left, right, ((0,), (0,)))[first:, :]


def lower_inverse(ref, size):
    for start in range(0, size, PANEL):
        stop = start + PANEL
        rows = ref[start:stop, :]
        lane = lax.broadcasted_iota(jnp.int32, rows.shape, 1)
        sub = lax.broadcasted_iota(jnp.int32, rows.shape, 0)
        inside = (lane >= start) & (lane < stop)
        eye = (lane == sub + start).astype(F32)
        (rows,) = eliminate((rows, [jnp.where(inside, eye, rows)]), start)
        ref[start:stop, :] = rows
        if stop < size:
            rest = ref[stop:, :]
            lane = lax.broadcasted_iota(jnp.int32, rest.shape, 1)
            rest = jnp.where((lane >= start) & (lane < stop), 0.0, rest)
            masked = rows
            ref[stop:, :] = rest - outer_rows(masked, stop)[: size - stop, :]


def factor_and_inverse(ref, size):
    for start in range(0, size, PANEL):
        stop = start + PANEL
        rows = ref[start:stop, :]
        (rows,) = eliminate((rows, [rows]), start)
        ref[start:stop, :] = rows
        if stop < size:
            ref[stop:, :] = ref[stop:, :] - outer_rows(rows, stop)[: size - stop, :]


def core_kernel(
    batch, updates, counts_ref, sum_ref, values_ref, basis_hbm, snaps_hbm, out_hbm, new_values_ref,
    gram, core, square, frame, big, small, coeff_ref, stack, result, basis_sem, snaps_sem, out_sem,
):
    rank = values_ref.shape[1]
    tiles, _, tile = stack.shape

    def tile_copies(i):
        return stack_copies(basis_hbm, snaps_hbm, stack, basis_sem, snaps_sem, i)

    def out_copy(i):
        spot = pl.ds(pl.multiple_of(i * tile, tile), tile)
        return pltpu.make_async_copy(result.at[i], out_hbm.at[:, spot], out_sem.at[i])

    def fetch(i, carry):
        for copy in tile_copies(i):
            copy.start()
        return carry

    lax.fori_loop(0, tiles, fetch, 0)
    width = gram.shape[0]
    rows = lax.broadcasted_iota(jnp.int32, (rank, rank), 0)
    lanes = lax.broadcasted_iota(jnp.int32, (rank, rank), 1)
    eye = rows == lanes
    count = sum_ref[0:1, rank - 1 : rank]
    wet_total = count * BLOCK
    parts = width // rank
    row = 0
    for i in range(parts):
        for j in range(i + 1):
            block = sum_ref[row : row + rank, :]
            row += rank
            if i == 0:
                block = jnp.where((rows == 0) & (lanes == rank - 1), block.T, block)
            gram[i * rank : (i + 1) * rank, j * rank : (j + 1) * rank] = block
            if i != j:
                gram[j * rank : (j + 1) * rank, i * rank : (i + 1) * rank] = block.T

    wide_rows = lax.broadcasted_iota(jnp.int32, (rank, width), 0)
    wide_lanes = lax.broadcasted_iota(jnp.int32, (rank, width), 1)
    start_frame = (wide_rows == wide_lanes).astype(F32)
    coeff_ref[...] = start_frame
    core[...] = jnp.zeros_like(core)
    diag = jnp.where(eye, values_ref[...], 0.0)

    batch_rows = lax.broadcasted_iota(jnp.int32, (batch, width), 0)
    batch_lanes = lax.broadcasted_iota(jnp.int32, (batch, width), 1)
    small_rows = lax.broadcasted_iota(jnp.int32, (batch, batch), 0)
    small_lanes = lax.broadcasted_iota(jnp.int32, (batch, batch), 1)

    for index in range(updates):
        coeff = coeff_ref[...]
        first = rank + index * batch
        projected = gram[:rank, :] if index == 0 else nn(coeff, gram[...])
        project = projected[:, first : first + batch] / wet_total
        picker = (batch_lanes == first + batch_rows).astype(F32)
        if index == 0:
            remain = picker - jnp.concatenate(
                [project.T, jnp.zeros((batch, width - rank), F32)], 1
            )
        else:
            remain = picker - tn(project, coeff)
        small[:, :batch] = nt(nn(remain, gram[...]), remain) / wet_total
        small[:, batch:] = (small_rows == small_lanes).astype(F32)
        factor_and_inverse(small, batch)
        factor_t = jnp.where(small_lanes >= small_rows, small[:, :batch], 0.0)
        fresh = nn(small[:, batch:], remain)
        core[:rank, :rank] = diag
        core[:rank, rank : rank + batch] = project
        core[rank : rank + batch, rank : rank + batch] = factor_t
        square[...] = self_nt(core[...])

        def sweep(step, carry):
            @pl.when(step == 0)
            def _():
                frame[...] = square[:rank, :]

            @pl.when(step > 0)
            def _():
                frame[...] = nn(frame[...], square[...])

            grown = frame[...]
            big[...] = self_nt(grown)
            lower_inverse(big, rank)
            inverse = jnp.where(lanes <= rows, big[...], 0.0)
            frame[...] = nn(inverse, grown)
            return carry

        lax.fori_loop(0, SWEEPS, sweep, 0)
        frame_now = frame[...]
        rotated = nn(frame_now, core[...])
        lengths = jnp.sqrt(jnp.sum(rotated * rotated, axis=1, keepdims=True))
        diag = jnp.where(eye, lengths, 0.0)
        if index == 0:
            carried = jnp.concatenate(
                [frame_now[:, :rank], jnp.zeros((rank, width - rank), F32)], 1
            )
        else:
            carried = nn(frame_now[:, :rank], coeff)
        coeff_ref[...] = carried + nn(frame_now[:, rank : rank + batch], fresh)
    new_values_ref[...] = jnp.sum(diag, axis=0, keepdims=True)

    coeff_high, coeff_low = split_two(coeff_ref[...])
    coeff_both = jnp.concatenate([coeff_high, coeff_low], 0)
    dims = ((1,), (0,))

    def apply(i, carry):
        for copy in tile_copies(i):
            copy.wait()
        high, low = masked_parts(counts_ref, stack, rank, i)
        both = dot_half(coeff_both, high, dims)
        result[i] = both[:rank, :] + (both[rank:, :] + dot_half(coeff_high, low, dims))
        out_copy(i).start()
        return carry

    lax.fori_loop(0, tiles, apply, 0)

    def drain(i, carry):
        out_copy(i).wait()
        return carry

    lax.fori_loop(0, tiles, drain, 0)


def per_device(groups, devs, basis_old, values_old, snapshots, wet_counts):
    rank, cells = basis_old.shape
    updates, batch = snapshots.shape[0], snapshots.shape[1]
    width = rank + updates * batch
    near = 1
    while (2 * near) * (2 * near) <= devs and devs % (2 * near) == 0:
        near *= 2
    far = devs // near
    members = groups * near
    parts = width // rank
    rows = rank * parts * (parts + 1) // 2
    chunk = -(-rows // (members * SUB)) * SUB
    padded = chunk * members
    tile = min(TILE, cells)

    tiles = cells // tile
    smem = pl.BlockSpec(memory_space=pltpu.SMEM)
    vmem = pl.BlockSpec(memory_space=pltpu.VMEM)
    hbm = pl.BlockSpec(memory_space=pl.ANY)
    summed = pl.pallas_call(
        functools.partial(gram_kernel, groups, near, far),
        out_shape=jax.ShapeDtypeStruct((padded, rank), F32),
        in_specs=[smem, hbm, hbm],
        out_specs=vmem,
        scratch_shapes=[
            pltpu.VMEM((tiles, width, tile), F32),
            pltpu.VMEM((width, width), F32),
            pltpu.VMEM((width, width), F32),
            pltpu.VMEM((padded, rank), F32),
            pltpu.VMEM((members, chunk, rank), F32),
            pltpu.VMEM((far, chunk, rank), F32),
            pltpu.VMEM((padded, rank), F32),
            pltpu.SemaphoreType.DMA((tiles,)),
            pltpu.SemaphoreType.DMA((updates, tiles)),
            pltpu.SemaphoreType.DMA((members,)),
            pltpu.SemaphoreType.DMA((members,)),
            pltpu.SemaphoreType.DMA((far,)),
            pltpu.SemaphoreType.DMA((far,)),
            pltpu.SemaphoreType.DMA((members,)),
            pltpu.SemaphoreType.DMA((members,)),
        ],
        compiler_params=pltpu.CompilerParams(
            collective_id=0, has_side_effects=True, vmem_limit_bytes=52 << 20
        ),
    )(wet_counts, basis_old, snapshots)

    basis_new, values = pl.pallas_call(
        functools.partial(core_kernel, batch, updates),
        out_shape=(
            jax.ShapeDtypeStruct((rank, cells), F32),
            jax.ShapeDtypeStruct((1, rank), F32),
        ),
        in_specs=[smem, vmem, vmem, hbm, hbm],
        out_specs=(hbm, vmem),
        scratch_shapes=[
            pltpu.VMEM((width, width), F32),
            pltpu.VMEM((width, width), F32),
            pltpu.VMEM((width, width), F32),
            pltpu.VMEM((rank, width), F32),
            pltpu.VMEM((rank, rank), F32),
            pltpu.VMEM((batch, 2 * batch), F32),
            pltpu.VMEM((rank, width), F32),
            pltpu.VMEM((tiles, width, tile), F32),
            pltpu.VMEM((tiles, rank, tile), F32),
            pltpu.SemaphoreType.DMA((tiles,)),
            pltpu.SemaphoreType.DMA((updates, tiles)),
            pltpu.SemaphoreType.DMA((tiles,)),
        ],
        compiler_params=pltpu.CompilerParams(vmem_limit_bytes=52 << 20),
    )(wet_counts, summed, values_old.reshape(1, rank), basis_old, snapshots)
    return basis_new, values.reshape(rank)


def solution(mesh):
    return jax.shard_map(
        functools.partial(per_device, mesh.shape["grp"], mesh.shape["dev"]),
        mesh=mesh,
        in_specs=(P(None, ("grp", "dev")), P(), P(None, None, ("grp", "dev")), P(("grp", "dev"))),
        out_specs=(P(None, ("grp", "dev")), P()),
        check_vma=False,
    )
```
